32 devices in a mesh: lat: 8 (over z, x), coh: 4 (over y, core).
Axes of the slice: x: 2, y: 2, z: 4, core: 2. Of those that a mesh axis runs over, the one named last changes fastest.
Arguments:
- density: float32 [128, 2, 64, 1024], P('coh', None, 'lat'), may hold values from 0.1 to 1
- cotangent: float32 [128, 2, 64, 1024], P('coh', None, 'lat'), may hold values from -0.5 to 1.5
- land_mask: int32 [2, 64, 1024], P(None, 'lat'), may hold values 0 or 1
- east_vel: float32 [2, 64, 1024], P(None, 'lat'), may hold values from -0.4 to 0.4
- north_vel: float32 [2, 64, 1024], P(None, 'lat'), may hold values from -0.4 to 0.4
- diffusion: float32 [2, 64, 1024], P(None, 'lat'), may hold values from 0.02 to 0.2
- age_class: int32 [128], P('coh'), may hold values from 0 to 31, as said below
- mort_rate: float32 [32], replicated, may hold values from 0.05 to 0.5
- crowd_coef: float32 [32], replicated, may hold values from 1 to 4
- mass: float32 [32], replicated, may hold values from 0.5 to 2
- speed: float32 [32], replicated, may hold values from 0.25 to 1
Outputs:
- grad_density: float32 [128, 2, 64, 1024], P('coh', None, 'lat')
- grad_east_vel: float32 [2, 64, 1024], P(None, 'lat', 'coh')
- grad_north_vel: float32 [2, 64, 1024], P(None, 'lat', 'coh')
- grad_diffusion: float32 [2, 64, 1024], P(None, 'lat', 'coh')
The draws below stay inside these ranges and needn't reach their ends.
Inputs may be any that keep to these rules, and one draw needn't show every extreme that they name: `age_class`: each age class is held by exactly 4 cohorts.
All inputs are finite; a program needn't handle non-finite values. No bound on the sum of `land_mask` on one device may be relied on, other than what follows from the above.
Results may differ from the reference program's by a relative error of at most 0.00014.
Values sent between devices are 32-bit elements; how exact they have to be, the bound alone decides.
A program may use at most 128 MiB of HBM per device.

```python
import math
import jax
import jax.numpy as jnp
from jax import lax

COH = 128
NAGE = 32
LAYERS = 2
STEPS = 2
LON = 1024
LAT = 64


def draw_age_class(key, part):
    shuffled = jax.random.permutation(key, COH)
    return (shuffled % NAGE).astype(jnp.int32)


def plant(values, stream_key, low, largest):
    longest = values.shape.index(max(values.shape))
    spots = []
    for shift in (0, 1):
        where = [jax.random.randint(jax.random.fold_in(stream_key, axis), (), 0, length) for axis, length in enumerate(values.shape)]
        where[longest] = (where[longest] + shift) % values.shape[longest]
        spots.append(tuple(where))
    return values.at[spots[0]].set(low).at[spots[1]].set(largest)


def level_of(rng, dims, split, smallest, largest):
    def one(position, shards_of):
        heights = jax.random.uniform(jax.random.fold_in(jax.random.fold_in(rng, 6), position), (shards_of,), jnp.float32, smallest / len(split), largest / len(split))
        return jnp.repeat(jnp.exp(heights), dims[position] // shards_of).reshape((-1,) + (1,) * (len(dims) - position - 1))

    level = one(*split[0])
    for cut in split[1:]:
        level = level * one(*cut)
    return level


def setup_inputs(seed: int = 0) -> dict:
    seeds = jax.random.split(jax.random.key(seed), 12)
    return {
        "density": jnp.clip(jnp.exp(math.log(1.0) - 2.3025851 * jax.random.uniform(seeds[0], (COH, LAYERS, LAT, LON), jnp.float32) ** level_of(seeds[0], (COH, LAYERS, LAT, LON), ((0, 4), (2, 8)), -0.2, 0.2)), 0.1, 1.0),
        "cotangent": jnp.clip(-0.5 + 2.0 * jax.random.uniform(seeds[1], (COH, LAYERS, LAT, LON), jnp.float32) ** level_of(seeds[1], (COH, LAYERS, LAT, LON), ((0, 4), (2, 8)), -0.2, 0.2), -0.5, 1.5),
        "land_mask": plant((jax.random.randint(seeds[2], (LAYERS, LAT, LON), 0, 8) < 7).astype(jnp.int32), jax.random.fold_in(seeds[2], 1), 0, 1),
        "east_vel": jnp.clip(jax.random.uniform(seeds[3], (LAYERS, LAT, LON), jnp.float32, -0.4, 0.4) * level_of(seeds[3], (LAYERS, LAT, LON), ((1, 8),), -0.4, 0.0), -0.4, 0.4),
        "north_vel": jnp.clip(jax.random.uniform(seeds[4], (LAYERS, LAT, LON), jnp.float32, -0.4, 0.4) * level_of(seeds[4], (LAYERS, LAT, LON), ((1, 8),), -0.4, 0.0), -0.4, 0.4),
        "diffusion": jnp.clip(0.02 + 0.18 * jax.random.uniform(seeds[5], (LAYERS, LAT, LON), jnp.float32) ** level_of(seeds[5], (LAYERS, LAT, LON), ((1, 8),), -0.2, 0.2), 0.02, 0.2),
        "age_class": draw_age_class(jax.random.fold_in(seeds[11], 71), 0),
        "mort_rate": jnp.clip(jnp.exp(jax.random.uniform(seeds[7], (NAGE,), jnp.float32, math.log(0.05), math.log(0.5))), 0.05, 0.5),
        "crowd_coef": jnp.clip(jnp.exp(jax.random.uniform(seeds[8], (NAGE,), jnp.float32, math.log(1.0), math.log(4.0))), 1.0, 4.0),
        "mass": jnp.clip(jnp.exp(jax.random.uniform(seeds[9], (NAGE,), jnp.float32, math.log(0.5), math.log(2.0))), 0.5, 2.0),
        "speed": jnp.clip(jnp.exp(jax.random.uniform(seeds[10], (NAGE,), jnp.float32, math.log(0.25), math.log(1.0))), 0.25, 1.0),
    }


def advance(state, ocean, east_vel, north_vel, diffusion, mortal, crowding, weight, swim):
    crowd = lax.optimization_barrier(jnp.sum(weight * state, axis=0)) / COH
    survival = jnp.exp(-(mortal + crowding * crowd[None]))
    survived = state * survival
    wet = ocean[None] * survived
    zero_row = jnp.zeros_like(wet[:, :, :1])
    north_val = jnp.concatenate([wet[:, :, 1:], zero_row], axis=2)
    south_val = jnp.concatenate([zero_row, wet[:, :, :-1]], axis=2)
    east_val = jnp.roll(wet, -1, axis=3)
    west_val = jnp.roll(wet, 1, axis=3)
    laplace = north_val + south_val + east_val + west_val - 4.0 * wet
    east_diff = 0.5 * (east_val - west_val)
    north_diff = 0.5 * (north_val - south_val)
    east_coef = swim * east_vel[None]
    north_coef = swim * north_vel[None]
    return ocean[None] * (wet + diffusion[None] * laplace - east_coef * east_diff - north_coef * north_diff)

def reference(density, cotangent, land_mask, east_vel, north_vel, diffusion, age_class, mort_rate, crowd_coef, mass, speed):
    ocean = land_mask.astype(density.dtype)
    mortal = mort_rate[age_class][:, None, None, None]
    crowding = crowd_coef[age_class][:, None, None, None]
    weight = mass[age_class][:, None, None, None]
    swim = speed[age_class][:, None, None, None]

    def forward(start, east_field, north_field, diff_field):

        def single(state):
            return advance(state, ocean, east_field, north_field, diff_field, mortal, crowding, weight, swim)
        stepper = jax.checkpoint(single)
        state = start
        for section in range(STEPS):
            state = stepper(state)
        return state
    final, pull = jax.vjp(forward, density, east_vel, north_vel, diffusion)
    grads = pull(cotangent)
    return (grads[0], grads[1], grads[2], grads[3])
```

```python
import functools

import jax
import jax.numpy as jnp
from jax import lax
from jax.experimental import pallas as pl
from jax.experimental.pallas import tpu as pltpu
from jax.sharding import PartitionSpec as P

STEPS = 2
MESH = pl.DeviceIdType.MESH
DENS, FIELDS, COT1, COT2, CROWD1, CROWD2, PRESS2, EDGE = range(8)
CENTRE, KAPPA, EAST, NORTH, OCEAN = range(5)


def rolled(value, by, axis):
    return pltpu.roll(value, by % value.shape[axis], axis)


def kernel(
    n_lat,
    n_coh,
    dens,
    cot,
    land,
    east,
    north,
    diff,
    age,
    mort,
    crowd_coef,
    mass,
    speed,
    out,
    out_east,
    out_north,
    out_kappa,
    field,
    halo_field,
    params,
    state,
    surv1,
    wet1,
    lap1,
    east1,
    north1,
    kept,
    total,
    partial,
    arrived,
    grads,
    share,
    share_in,
    dens_o,
    dens_h,
    field_o,
    field_h,
    cot1_o,
    cot1_h,
    cot2_o,
    cot2_h,
    sums_o,
    sums_h,
    edge_o,
    edge_h,
    wet_edge,
    into,
    kept_h,
    lat_send,
    lat_recv,
    coh_send,
    coh_recv,
    share_send,
    share_recv,
):
    cohorts, layers, rows, lon = dens.shape
    every = cohorts * n_coh
    lat = lax.axis_index("lat")
    coh = lax.axis_index("coh")
    has_low = lat > 0
    has_high = lat < n_lat - 1
    low = jnp.maximum(lat - 1, 0)
    high = jnp.minimum(lat + 1, n_lat - 1)
    peers = [lax.rem(coh + by, n_coh) for by in range(1, n_coh)]

    barrier = pltpu.get_barrier_semaphore()
    for peer in peers:
        pl.semaphore_signal(barrier, inc=1, device_id={"coh": peer}, device_id_type=MESH)

    @pl.when(has_low)
    def _():
        pl.semaphore_signal(barrier, inc=1, device_id={"lat": low}, device_id_type=MESH)

    @pl.when(has_high)
    def _():
        pl.semaphore_signal(barrier, inc=1, device_id={"lat": high}, device_id_type=MESH)

    def copies(kind, outgoing, incoming):
        def one(side, device):
            return pltpu.make_async_remote_copy(
                src_ref=outgoing.at[side],
                dst_ref=incoming.at[1 - side],
                send_sem=lat_send.at[kind, side],
                recv_sem=lat_recv.at[kind, 1 - side],
                device_id={"lat": device},
                device_id_type=MESH,
            )

        return one(0, low), one(1, high)

    messages = {
        DENS: copies(DENS, dens_o, dens_h),
        FIELDS: copies(FIELDS, field_o, field_h),
        COT1: copies(COT1, cot1_o, cot1_h),
        COT2: copies(COT2, cot2_o, cot2_h),
        CROWD1: copies(CROWD1, sums_o.at[0], sums_h.at[0]),
        CROWD2: copies(CROWD2, sums_o.at[1], sums_h.at[1]),
        PRESS2: copies(PRESS2, sums_o.at[2], sums_h.at[2]),
        EDGE: copies(EDGE, edge_o, edge_h),
    }

    def send(kind):
        to_low, to_high = messages[kind]

        @pl.when(has_low)
        def _():
            to_low.start()

        @pl.when(has_high)
        def _():
            to_high.start()

    def receive(kind):
        to_low, to_high = messages[kind]

        @pl.when(has_low)
        def _():
            to_high.wait_recv()

        @pl.when(has_high)
        def _():
            to_low.wait_recv()

    def sent(kind):
        to_low, to_high = messages[kind]

        @pl.when(has_low)
        def _():
            to_low.wait_send()

        @pl.when(has_high)
        def _():
            to_high.wait_send()

    def exchange(which):
        return [
            pltpu.make_async_remote_copy(
                src_ref=partial.at[which],
                dst_ref=arrived.at[which, by],
                send_sem=coh_send.at[which, by],
                recv_sem=coh_recv.at[which, by],
                device_id={"coh": peer},
                device_id_type=MESH,
            )
            for by, peer in enumerate(peers)
        ]

    def summed(which):
        for copy in exchange(which):
            copy.wait_recv()
        for layer in range(layers):
            value = partial[which, layer]
            for by in range(n_coh - 1):
                value = value + arrived[which, by, layer]
            total[which, layer] = value * (1.0 / every)

    def pass_sums(which, kind):
        for layer in range(layers):
            value = total[which, layer]
            sums_o[which, 0, layer : layer + 1] = value[:1]
            sums_o[which, 1, layer : layer + 1] = value[rows - 1 :]
        send(kind)

    def pack(source, low_row, high_row, target):
        def body(cohort, carry):
            for layer in range(layers):
                spot = pl.ds(layer * cohorts + cohort, 1)
                target[0, spot, :] = source[cohort, layer, low_row : low_row + 1, :]
                target[1, spot, :] = source[cohort, layer, high_row : high_row + 1, :]
            return carry

        lax.fori_loop(0, cohorts, body, 0)

    pack(dens, 0, rows - 1, dens_o)
    for layer in range(layers):
        raw = (land[layer].astype(jnp.float32), east[layer], north[layer], diff[layer])
        for index, value in enumerate(raw):
            for depth in range(2):
                spot = slice(depth * layers + layer, depth * layers + layer + 1)
                field_o[0, index, spot, :] = value[depth : depth + 1]
                field_o[1, index, spot, :] = value[rows - 1 - depth : rows - depth]
    nobody = jnp.logical_not

    @pl.when(nobody(has_low))
    def _():
        for target in (dens_h, field_h, cot1_h, cot2_h, edge_h):
            target[0] = jnp.zeros(target.shape[1:], jnp.float32)
        for which in range(3):
            sums_h[which, 0] = jnp.zeros(sums_h.shape[2:], jnp.float32)

    @pl.when(nobody(has_high))
    def _():
        for target in (dens_h, field_h, cot1_h, cot2_h, edge_h):
            target[1] = jnp.zeros(target.shape[1:], jnp.float32)
        for which in range(3):
            sums_h[which, 1] = jnp.zeros(sums_h.shape[2:], jnp.float32)

    pl.semaphore_wait(
        barrier, n_coh - 1 + has_low.astype(jnp.int32) + has_high.astype(jnp.int32)
    )
    send(DENS)
    send(FIELDS)

    def weigh(cohort, sums):
        weight = mass[age[cohort]]
        return tuple(sums[layer] + weight * dens[cohort, layer] for layer in range(layers))

    zero = jnp.zeros((rows, lon), jnp.float32)
    sums = lax.fori_loop(0, cohorts, weigh, (zero,) * layers)
    for layer in range(layers):
        partial[0, layer] = sums[layer]
    for copy in exchange(0):
        copy.start()

    for layer in range(layers):
        ocean = land[layer].astype(jnp.float32)
        kappa = diff[layer]
        field[CENTRE, layer] = ocean * (1.0 - 4.0 * kappa)
        field[KAPPA, layer] = ocean * kappa
        field[EAST, layer] = ocean * (0.5 * east[layer])
        field[NORTH, layer] = ocean * (0.5 * north[layer])
        field[OCEAN, layer] = ocean
    for cohort in range(cohorts):
        one = age[cohort]
        for index, table in enumerate((mort, crowd_coef, mass, speed)):
            params[index, cohort : cohort + 1, :] = jnp.full((1, 128), table[one], jnp.float32)
    pack(cot, 0, rows - 1, cot1_o)
    pack(cot, 1, rows - 2, cot2_o)
    grads[...] = jnp.zeros(grads.shape, jnp.float32)

    summed(0)
    pass_sums(0, CROWD1)
    send(COT1)

    def wide(index, first):
        value = params[index, pl.ds(first, 8), :]
        return jnp.concatenate([value] * (lon // 128), axis=1)

    def spread(row):
        return jnp.broadcast_to(row, (8, lon))

    def over_groups(body):
        def one(group, carry):
            first = pl.multiple_of(group * 8, 8)
            for layer in range(layers):
                spot = pl.ds(pl.multiple_of(layer * cohorts + first, 8), 8)
                body(first, layer, spot)
            return carry

        lax.fori_loop(0, cohorts // 8, one, 0)

    def halo_row(side, index, depth, layer):
        spot = depth * layers + layer
        return spread(halo_field[side, index, spot : spot + 1, :])

    receive(FIELDS)
    for side in range(2):
        ocean = field_h[side, 0]
        kappa = field_h[side, 3]
        halo_field[side, CENTRE] = ocean * (1.0 - 4.0 * kappa)
        halo_field[side, KAPPA] = ocean * kappa
        halo_field[side, EAST] = ocean * (0.5 * field_h[side, 1])
        halo_field[side, NORTH] = ocean * (0.5 * field_h[side, 2])
        halo_field[side, OCEAN] = ocean

    def survival_h(side, which, first, layer):
        crowd = spread(sums_h[which, side, layer : layer + 1, :])
        return halo_row(side, OCEAN, 0, layer) * jnp.exp(-(wide(0, first) + wide(1, first) * crowd))

    receive(CROWD1)
    receive(DENS)

    def wet_halo(first, layer, spot):
        for side in range(2):
            into[side, spot, :] = dens_h[side, spot, :] * survival_h(side, 0, first, layer)

    over_groups(wet_halo)

    row = lax.broadcasted_iota(jnp.int32, (rows, lon), 0)
    is_first = row == 0
    is_last = row == rows - 1

    def from_before(value, edge):
        return jnp.where(is_first, edge, rolled(value, 1, 0))

    def from_after(value, edge):
        return jnp.where(is_last, edge, rolled(value, -1, 0))

    def scalars(cohort):
        one = age[cohort]
        return mort[one], crowd_coef[one], mass[one], speed[one]

    def survival(layer, which, mortal, crowding):
        return field[OCEAN, layer] * jnp.exp(-(mortal + crowding * total[which, layer]))

    def forward(cohort, sums):
        mortal, crowding, weight, swim = scalars(cohort)
        added = []
        for layer in range(layers):
            spot = pl.ds(layer * cohorts + cohort, 1)
            alive = survival(layer, 0, mortal, crowding)
            wet = dens[cohort, layer] * alive
            before = from_before(wet, into[0, spot, :])
            after = from_after(wet, into[1, spot, :])
            west_val = rolled(wet, 1, 1)
            east_val = rolled(wet, -1, 1)
            around = (before + after) + (west_val + east_val)
            east_diff = east_val - west_val
            north_diff = after - before
            value = (
                field[CENTRE, layer] * wet
                + field[KAPPA, layer] * around
                - swim * (field[EAST, layer] * east_diff + field[NORTH, layer] * north_diff)
            )
            surv1[cohort, layer] = alive
            wet1[cohort, layer] = wet
            lap1[cohort, layer] = around - 4.0 * wet
            east1[cohort, layer] = east_diff
            north1[cohort, layer] = north_diff
            state[cohort, layer] = value
            added.append(sums[layer] + weight * value)
        return tuple(added)

    sums = lax.fori_loop(0, cohorts, forward, (zero,) * layers)
    for layer in range(layers):
        partial[1, layer] = sums[layer]
    for copy in exchange(1):
        copy.start()
    send(COT2)

    def flow_in(adjoint, target):
        def body(first, layer, spot):
            swim = wide(3, first)
            for side in range(2):
                shift = swim * halo_row(side, NORTH, 0, layer)
                kappa = halo_row(side, KAPPA, 0, layer)
                coef = kappa - shift if side == 0 else kappa + shift
                target[side, spot, :] = coef * adjoint(side, first, layer, spot)

        over_groups(body)

    receive(COT1)
    flow_in(lambda side, first, layer, spot: cot1_h[side, spot, :], into)
    summed(1)
    pass_sums(1, CROWD2)

    def pulled(adjoint, swum, layer, edges):
        spread_out = field[KAPPA, layer] * adjoint
        drift = field[EAST, layer] * swum
        climb = field[NORTH, layer] * swum
        return (
            field[CENTRE, layer] * adjoint
            + rolled(spread_out - drift, 1, 1)
            + rolled(spread_out + drift, -1, 1)
            + from_before(spread_out - climb, edges[0])
            + from_after(spread_out + climb, edges[1])
        )

    def back2(cohort, sums):
        mortal, crowding, weight, swim = scalars(cohort)
        added = []
        for layer in range(layers):
            spot = pl.ds(layer * cohorts + cohort, 1)
            alive = survival(layer, 1, mortal, crowding)
            wet = state[cohort, layer] * alive
            wet_edge[0, spot, :] = wet[:1]
            wet_edge[1, spot, :] = wet[rows - 1 :]
            before = from_before(wet, 0.0)
            after = from_after(wet, 0.0)
            west_val = rolled(wet, 1, 1)
            east_val = rolled(wet, -1, 1)
            adjoint = cot[cohort, layer]
            swum = swim * adjoint
            grads[0, layer] += swum * (east_val - west_val)
            grads[1, layer] += swum * (after - before)
            grads[2, layer] += adjoint * (
                (before + after) + (west_val + east_val) - 4.0 * wet
            )
            pull = pulled(adjoint, swum, layer, (into[0, spot, :], into[1, spot, :]))
            kept[cohort, layer] = pull * alive
            added.append(sums[layer] - crowding * (pull * wet))
        return tuple(added)

    sums = lax.fori_loop(0, cohorts, back2, (zero,) * layers)
    for layer in range(layers):
        partial[2, layer] = sums[layer]
    for copy in exchange(2):
        copy.start()

    edge_o[...] = jnp.zeros(edge_o.shape, jnp.float32)

    def products(first, layer, spot):
        swim = wide(3, first)
        for side in range(2):
            product = cot1_h[side, spot, :] * wet_edge[side, spot, :]
            edge_o[side, layer] += product
            edge_o[side, layers + layer] += swim * product

    over_groups(products)
    send(EDGE)

    receive(CROWD2)
    receive(COT2)

    def back2_halo(first, layer, spot):
        swim = wide(3, first)
        for side in range(2):
            sign = 1.0 if side == 0 else -1.0
            adjoint = cot1_h[side, spot, :]
            inner = 0 if side == 0 else rows - 1
            spread_out = halo_row(side, KAPPA, 0, layer) * adjoint
            drift = halo_row(side, EAST, 0, layer) * swim * adjoint
            outer_coef = halo_row(side, KAPPA, 1, layer) - sign * swim * halo_row(side, NORTH, 1, layer)
            inner_coef = spread(field[KAPPA, layer, inner : inner + 1, :]) + sign * swim * spread(
                field[NORTH, layer, inner : inner + 1, :]
            )
            pull = (
                halo_row(side, CENTRE, 0, layer) * adjoint
                + rolled(spread_out - drift, 1, 1)
                + rolled(spread_out + drift, -1, 1)
                + outer_coef * cot2_h[side, spot, :]
                + inner_coef * cot1_o[side, spot, :]
            )
            kept_h[side, spot, :] = pull * survival_h(side, 1, first, layer)

    over_groups(back2_halo)

    summed(2)
    pass_sums(2, PRESS2)
    receive(PRESS2)
    flow_in(
        lambda side, first, layer, spot: kept_h[side, spot, :]
        + wide(2, first) * spread(sums_h[2, side, layer : layer + 1, :]),
        into,
    )

    def back1(cohort, sums):
        mortal, crowding, weight, swim = scalars(cohort)
        added = []
        for layer in range(layers):
            spot = pl.ds(layer * cohorts + cohort, 1)
            adjoint = kept[cohort, layer] + weight * total[2, layer]
            swum = swim * adjoint
            grads[0, layer] += swum * east1[cohort, layer]
            grads[1, layer] += swum * north1[cohort, layer]
            grads[2, layer] += adjoint * lap1[cohort, layer]
            pull = pulled(adjoint, swum, layer, (into[0, spot, :], into[1, spot, :]))
            out[cohort, layer] = pull * surv1[cohort, layer]
            added.append(sums[layer] - crowding * (pull * wet1[cohort, layer]))
        return tuple(added)

    sums = lax.fori_loop(0, cohorts, back1, (zero,) * layers)
    for layer in range(layers):
        partial[3, layer] = sums[layer]
    for copy in exchange(3):
        copy.start()

    receive(EDGE)
    part = lon // n_coh
    for layer in range(layers):
        ocean = field[OCEAN, layer]
        sums = [jnp.sum(edge_h[side, layer], axis=0, keepdims=True) for side in range(2)]
        swims = [jnp.sum(edge_h[side, layers + layer], axis=0, keepdims=True) for side in range(2)]
        kappa = grads[2, layer] + jnp.where(is_first, sums[0], 0.0) + jnp.where(is_last, sums[1], 0.0)
        climb = grads[1, layer] + jnp.where(is_last, swims[1], 0.0) - jnp.where(is_first, swims[0], 0.0)
        values = (-0.5 * ocean * grads[0, layer], -0.5 * ocean * climb, ocean * kappa)
        for index, value in enumerate(values):
            for to in range(n_coh):
                share[to, index, layer] = value[:, to * part : (to + 1) * part]
    shares = [
        pltpu.make_async_remote_copy(
            src_ref=share.at[peer],
            dst_ref=share_in.at[by],
            send_sem=share_send.at[by],
            recv_sem=share_recv.at[by],
            device_id={"coh": peer},
            device_id_type=MESH,
        )
        for by, peer in enumerate(peers)
    ]
    for copy in shares:
        copy.start()

    summed(3)

    def finish(cohort, carry):
        weight = mass[age[cohort]]
        for layer in range(layers):
            out[cohort, layer] += weight * total[3, layer]
        return carry

    lax.fori_loop(0, cohorts, finish, 0)

    for copy in shares:
        copy.wait_recv()
    for index, target in enumerate((out_east, out_north, out_kappa)):
        value = share[coh, index]
        for by in range(n_coh - 1):
            value = value + share_in[by, index]
        target[...] = value

    for kind in messages:
        sent(kind)
    for which in range(2 * STEPS):
        for copy in exchange(which):
            copy.wait_send()
    for copy in shares:
        copy.wait_send()


def local(*args):
    density = args[0]
    cohorts, layers, rows, lon = density.shape
    n_lat, n_coh = lax.axis_size("lat"), lax.axis_size("coh")
    f32 = jnp.float32
    vmem = pl.BlockSpec(memory_space=pltpu.VMEM)
    smem = pl.BlockSpec(memory_space=pltpu.SMEM)
    share = jax.ShapeDtypeStruct((layers, rows, lon // n_coh), f32)
    whole = pltpu.VMEM(density.shape, f32)
    packed = pltpu.VMEM((2, layers * cohorts, lon), f32)
    scratch = [
        pltpu.VMEM((5, layers, rows, lon), f32),
        pltpu.VMEM((2, 5, 2 * layers, lon), f32),
        pltpu.VMEM((4, cohorts, 128), f32),
        whole,
        whole,
        whole,
        whole,
        whole,
        whole,
        whole,
        pltpu.VMEM((4, layers, rows, lon), f32),
        pltpu.VMEM((4, layers, rows, lon), f32),
        pltpu.VMEM((4, n_coh - 1, layers, rows, lon), f32),
        pltpu.VMEM((3, layers, rows, lon), f32),
        pltpu.VMEM((n_coh, 3, layers, rows, lon // n_coh), f32),
        pltpu.VMEM((n_coh - 1, 3, layers, rows, lon // n_coh), f32),
        packed,
        packed,
        pltpu.VMEM((2, 4, 2 * layers, lon), f32),
        pltpu.VMEM((2, 4, 2 * layers, lon), f32),
        packed,
        packed,
        packed,
        packed,
        pltpu.VMEM((3, 2, layers, lon), f32),
        pltpu.VMEM((3, 2, layers, lon), f32),
        pltpu.VMEM((2, 2 * layers, 8, lon), f32),
        pltpu.VMEM((2, 2 * layers, 8, lon), f32),
        packed,
        packed,
        packed,
        pltpu.SemaphoreType.DMA((8, 2)),
        pltpu.SemaphoreType.DMA((8, 2)),
        pltpu.SemaphoreType.DMA((4, n_coh - 1)),
        pltpu.SemaphoreType.DMA((4, n_coh - 1)),
        pltpu.SemaphoreType.DMA((n_coh - 1,)),
        pltpu.SemaphoreType.DMA((n_coh - 1,)),
    ]
    return pl.pallas_call(
        functools.partial(kernel, n_lat, n_coh),
        out_shape=(jax.ShapeDtypeStruct(density.shape, f32), share, share, share),
        in_specs=[vmem] * 6 + [smem] * 5,
        out_specs=(vmem,) * 4,
        scratch_shapes=scratch,
        compiler_params=pltpu.CompilerParams(
            collective_id=0, has_side_effects=True, vmem_limit_bytes=56 * 1024 * 1024
        ),
        cost_estimate=pl.CostEstimate(
            flops=150 * density.size, bytes_accessed=12 * density.size, transcendentals=2 * density.size
        ),
    )(*args)


def solution(mesh):
    fields = P(None, "lat", None)
    in_specs = (P("coh", None, "lat", None),) * 2 + (fields,) * 4 + (P("coh"),) + (P(),) * 4
    out_specs = (P("coh", None, "lat", None),) + (P(None, "lat", "coh"),) * 3
    return jax.shard_map(local, mesh=mesh, in_specs=in_specs, out_specs=out_specs, check_vma=False)
```

```python
import functools

import jax
import jax.numpy as jnp
from jax import lax
from jax.experimental import pallas as pl
from jax.experimental.pallas import tpu as pltpu
from jax.sharding import PartitionSpec as P

STEPS = 2
MESH = pl.DeviceIdType.MESH
FIELDS, COT1, COT2, PART2, CROWD2, PRESS2, EDGE = range(7)
KAPPA_NEAR, NORTH_NEAR, EAST_NEAR, KAPPA_FAR, NORTH_FAR, KAPPA_OWN, NORTH_OWN = range(7)
SENT = 5
CENTRE, KAPPA, EAST, NORTH, OCEAN = range(5)


def rolled(value, by, axis):
    return pltpu.roll(value, by % value.shape[axis], axis)


def kernel(
    n_lat,
    n_coh,
    dens_in,
    cot_in,
    land,
    east,
    north,
    diff,
    age,
    mort,
    crowd_coef,
    mass,
    speed,
    out,
    out_press,
    out_grads,
    dens,
    cot,
    last,
    field,
    halo_field,
    params,
    state,
    surv1,
    wet1,
    lap1,
    east1,
    north1,
    kept,
    total,
    partial,
    arrived,
    grads,
    share,
    share_in,
    dens_edge,
    field_o,
    field_h,
    cot1_o,
    cot1_h,
    cot2_o,
    cot2_h,
    sums_o,
    sums_h,
    press_o,
    press_h,
    edge_o,
    edge_h,
    edge_sum,
    beyond,
    beyond_o,
    beyond_in,
    wet_edge,
    wet1_edge,
    coefs,
    inflow,
    into,
    kept_h,
    local_sem,
    lat_send,
    lat_recv,
    coh_send,
    coh_recv,
    share_send,
    share_recv,
):
    cohorts, layers, rows, lon = dens.shape
    get_cot = pltpu.make_async_copy(cot_in, cot, local_sem.at[0])
    get_dens = pltpu.make_async_copy(dens_in, dens, local_sem.at[1])
    get_cot.start()
    get_dens.start()
    every = cohorts * n_coh
    lat = lax.axis_index("lat")
    coh = lax.axis_index("coh")
    has_low = lat > 0
    has_high = lat < n_lat - 1
    low = jnp.maximum(lat - 1, 0)
    high = jnp.minimum(lat + 1, n_lat - 1)
    peers = [lax.rem(coh + by, n_coh) for by in range(1, n_coh)]

    barrier = pltpu.get_barrier_semaphore()
    for peer in peers:
        pl.semaphore_signal(barrier, inc=1, device_id={"coh": peer}, device_id_type=MESH)

    @pl.when(has_low)
    def _():
        pl.semaphore_signal(barrier, inc=1, device_id={"lat": low}, device_id_type=MESH)

    @pl.when(has_high)
    def _():
        pl.semaphore_signal(barrier, inc=1, device_id={"lat": high}, device_id_type=MESH)

    def copies(kind, outgoing, incoming):
        def one(side, device):
            return pltpu.make_async_remote_copy(
                src_ref=outgoing.at[side],
                dst_ref=incoming.at[1 - side],
                send_sem=lat_send.at[kind, side],
                recv_sem=lat_recv.at[kind, 1 - side],
                device_id={"lat": device},
                device_id_type=MESH,
            )

        return one(0, low), one(1, high)

    messages = {
        FIELDS: copies(FIELDS, field_o, field_h),
        COT1: copies(COT1, cot1_o, cot1_h),
        COT2: copies(COT2, cot2_o, cot2_h),
        PART2: copies(PART2, sums_o.at[0], sums_h.at[0]),
        CROWD2: copies(CROWD2, sums_o.at[1], sums_h.at[1]),
        PRESS2: copies(PRESS2, press_o, press_h),
        EDGE: copies(EDGE, edge_o, edge_h),
    }

    def send(kind):
        to_low, to_high = messages[kind]

        @pl.when(has_low)
        def _():
            to_low.start()

        @pl.when(has_high)
        def _():
            to_high.start()

    def receive(kind):
        to_low, to_high = messages[kind]

        @pl.when(has_low)
        def _():
            to_high.wait_recv()

        @pl.when(has_high)
        def _():
            to_low.wait_recv()

    def sent(kind):
        to_low, to_high = messages[kind]

        @pl.when(has_low)
        def _():
            to_low.wait_send()

        @pl.when(has_high)
        def _():
            to_high.wait_send()

    def exchange(which):
        return [
            pltpu.make_async_remote_copy(
                src_ref=partial.at[which],
                dst_ref=arrived.at[which, by],
                send_sem=coh_send.at[which, by],
                recv_sem=coh_recv.at[which, by],
                device_id={"coh": peer},
                device_id_type=MESH,
            )
            for by, peer in enumerate(peers)
        ]

    def summed(which):
        for copy in exchange(which):
            copy.wait_recv()
        for layer in range(layers):
            value = partial[which, layer]
            for by in range(n_coh - 1):
                value = value + arrived[which, by, layer]
            total[which, layer] = value * (1.0 / every)

    def pack(source, low_row, high_row, target):
        def body(cohort, carry):
            for layer in range(layers):
                spot = pl.ds(layer * cohorts + cohort, 1)
                target[0, spot, :] = source[cohort, layer, low_row : low_row + 1, :]
                target[1, spot, :] = source[cohort, layer, high_row : high_row + 1, :]
            return carry

        lax.fori_loop(0, cohorts, body, 0)

    for layer in range(layers):
        raw = (land[layer].astype(jnp.float32), east[layer], north[layer], diff[layer])
        for index, value in enumerate(raw):
            for depth in range(2):
                spot = slice(depth * layers + layer, depth * layers + layer + 1)
                field_o[0, index, spot, :] = value[depth : depth + 1]
                field_o[1, index, spot, :] = value[rows - 1 - depth : rows - depth]

    for side, exists in ((0, has_low), (1, has_high)):

        @pl.when(jnp.logical_not(exists))
        def _(side=side):
            for target in (field_h, cot1_h, cot2_h, press_h, edge_h):
                target[side] = jnp.zeros(target.shape[1:], jnp.float32)
            for which in range(2):
                sums_h[which, side] = jnp.zeros(sums_h.shape[2:], jnp.float32)

    get_cot.wait()
    pack(cot, 0, rows - 1, cot1_o)
    pl.semaphore_wait(
        barrier, n_coh - 1 + has_low.astype(jnp.int32) + has_high.astype(jnp.int32)
    )
    send(COT1)
    send(FIELDS)
    get_dens.wait()

    def weigh(cohort, sums):
        weight = mass[age[cohort]]
        return tuple(sums[layer] + weight * dens[cohort, layer] for layer in range(layers))

    zero = jnp.zeros((rows, lon), jnp.float32)
    sums = lax.fori_loop(0, cohorts, weigh, (zero,) * layers)
    for layer in range(layers):
        partial[0, layer] = sums[layer]
    for copy in exchange(0):
        copy.start()

    for layer in range(layers):
        ocean = land[layer].astype(jnp.float32)
        kappa = diff[layer]
        field[CENTRE, layer] = ocean * (1.0 - 4.0 * kappa)
        field[KAPPA, layer] = ocean * kappa
        field[EAST, layer] = ocean * (0.5 * east[layer])
        field[NORTH, layer] = ocean * (0.5 * north[layer])
        field[OCEAN, layer] = ocean
    for cohort in range(cohorts):
        one = age[cohort]
        for index, table in enumerate((mort, crowd_coef, mass, speed)):
            params[index, cohort : cohort + 1, :] = jnp.full((1, 128), table[one], jnp.float32)
    pack(cot, 1, rows - 2, cot2_o)
    send(COT2)
    pack(dens, 0, rows - 1, dens_edge)
    grads[...] = jnp.zeros(grads.shape, jnp.float32)
    edge_sum[...] = jnp.zeros(edge_sum.shape, jnp.float32)
    beyond[...] = jnp.zeros(beyond.shape, jnp.float32)

    def wide(index, first):
        value = params[index, pl.ds(first, 8), :]
        return jnp.concatenate([value] * (lon // 128), axis=1)

    def spread(row):
        return jnp.broadcast_to(row, (8, lon))

    def over_groups(body):
        def one(group, carry):
            first = pl.multiple_of(group * 8, 8)
            for layer in range(layers):
                spot = pl.ds(pl.multiple_of(layer * cohorts + first, 8), 8)
                body(first, layer, spot)
            return carry

        lax.fori_loop(0, cohorts // 8, one, 0)

    def halo_row(side, index, depth, layer):
        spot = depth * layers + layer
        return spread(halo_field[side, index, spot : spot + 1, :])

    receive(FIELDS)
    for side in range(2):
        ocean = field_h[side, 0]
        kappa = field_h[side, 3]
        halo_field[side, CENTRE] = ocean * (1.0 - 4.0 * kappa)
        halo_field[side, KAPPA] = ocean * kappa
        halo_field[side, EAST] = ocean * (0.5 * field_h[side, 1])
        halo_field[side, NORTH] = ocean * (0.5 * field_h[side, 2])
        halo_field[side, OCEAN] = ocean

    def survival_h(side, which, first, layer):
        crowd = spread(sums_h[which, side, layer : layer + 1, :])
        return halo_row(side, OCEAN, 0, layer) * jnp.exp(-(wide(0, first) + wide(1, first) * crowd))

    def inner(side):
        return slice(0, 1) if side == 0 else slice(rows - 1, rows)

    def column(value):
        return jnp.sum(value, axis=0, keepdims=True)

    summed(0)

    def outflow(first, layer, spot):
        swim = wide(3, first)
        for side in range(2):
            crowd = spread(total[0, layer, inner(side), :])
            ocean = spread(field[OCEAN, layer, inner(side), :])
            wet = dens_edge[side, spot, :] * (ocean * jnp.exp(-(wide(0, first) + wide(1, first) * crowd)))
            shift = swim * halo_row(side, NORTH, 0, layer)
            kappa = halo_row(side, KAPPA, 0, layer)
            coef = kappa - shift if side == 0 else kappa + shift
            value = coef * wet
            wet1_edge[side, spot, :] = wet
            coefs[side, spot, :] = coef
            inflow[side, spot, :] = value
            beyond[0, side, layer] += wide(2, first) * value

    over_groups(outflow)
    for side in range(2):
        for layer in range(layers):
            sums_o[0, side, layer : layer + 1] = column(beyond[0, side, layer])
    send(PART2)

    row = lax.broadcasted_iota(jnp.int32, (rows, lon), 0)
    is_first = row == 0
    is_last = row == rows - 1

    def from_before(value, edge):
        return jnp.where(is_first, edge, rolled(value, 1, 0))

    def from_after(value, edge):
        return jnp.where(is_last, edge, rolled(value, -1, 0))

    def scalars(cohort):
        one = age[cohort]
        return mort[one], crowd_coef[one], mass[one], speed[one]

    def survival(layer, which, mortal, crowding):
        return field[OCEAN, layer] * jnp.exp(-(mortal + crowding * total[which, layer]))

    def forward(cohort, sums):
        mortal, crowding, weight, swim = scalars(cohort)
        added = []
        for layer in range(layers):
            alive = survival(layer, 0, mortal, crowding)
            wet = dens[cohort, layer] * alive
            before = from_before(wet, 0.0)
            after = from_after(wet, 0.0)
            west_val = rolled(wet, 1, 1)
            east_val = rolled(wet, -1, 1)
            around = (before + after) + (west_val + east_val)
            east_diff = east_val - west_val
            north_diff = after - before
            value = (
                field[CENTRE, layer] * wet
                + field[KAPPA, layer] * around
                - swim * (field[EAST, layer] * east_diff + field[NORTH, layer] * north_diff)
            )
            surv1[cohort, layer] = alive
            wet1[cohort, layer] = wet
            lap1[cohort, layer] = around - 4.0 * wet
            east1[cohort, layer] = east_diff
            north1[cohort, layer] = north_diff
            state[cohort, layer] = value
            added.append(sums[layer] + weight * value)
        return tuple(added)

    sums = lax.fori_loop(0, cohorts, forward, (zero,) * layers)
    receive(PART2)
    for layer in range(layers):
        partial[1, layer] = sums[layer] + (
            jnp.where(is_first, sums_h[0, 0, layer : layer + 1, :], 0.0)
            + jnp.where(is_last, sums_h[0, 1, layer : layer + 1, :], 0.0)
        )
    for copy in exchange(1):
        copy.start()

    receive(COT1)

    def inflow_cot(first, layer, spot):
        for side in range(2):
            into[side, spot, :] = coefs[side, spot, :] * cot1_h[side, spot, :]

    over_groups(inflow_cot)
    summed(1)
    for side in range(2):
        for layer in range(layers):
            sums_o[1, side, layer : layer + 1] = total[1, layer, inner(side), :]
    send(CROWD2)

    def pulled(adjoint, swum, layer, edges):
        spread_out = field[KAPPA, layer] * adjoint
        drift = field[EAST, layer] * swum
        climb = field[NORTH, layer] * swum
        return (
            field[CENTRE, layer] * adjoint
            + rolled(spread_out - drift, 1, 1)
            + rolled(spread_out + drift, -1, 1)
            + from_before(spread_out - climb, edges[0])
            + from_after(spread_out + climb, edges[1])
        )

    def back2(cohort, sums):
        mortal, crowding, weight, swim = scalars(cohort)
        added = []
        for layer in range(layers):
            spot = pl.ds(layer * cohorts + cohort, 1)
            alive = survival(layer, 1, mortal, crowding)
            wet = state[cohort, layer] * alive
            wet_edge[0, spot, :] = wet[:1]
            wet_edge[1, spot, :] = wet[rows - 1 :]
            before = from_before(wet, 0.0)
            after = from_after(wet, 0.0)
            west_val = rolled(wet, 1, 1)
            east_val = rolled(wet, -1, 1)
            adjoint = cot[cohort, layer]
            swum = swim * adjoint
            grads[0, layer] += swum * (east_val - west_val)
            grads[1, layer] += swum * (after - before)
            grads[2, layer] += adjoint * (
                (before + after) + (west_val + east_val) - 4.0 * wet
            )
            pull = pulled(adjoint, swum, layer, (into[0, spot, :], into[1, spot, :]))
            kept[cohort, layer] = pull * alive
            added.append(sums[layer] - crowding * (pull * wet))
        return tuple(added)

    sums = lax.fori_loop(0, cohorts, back2, (zero,) * layers)
    for layer in range(layers):
        partial[2, layer] = sums[layer]
    for copy in exchange(2):
        copy.start()

    receive(CROWD2)
    receive(COT2)

    def back2_halo(first, layer, spot):
        swim = wide(3, first)
        for side in range(2):
            sign = 1.0 if side == 0 else -1.0
            adjoint = cot1_h[side, spot, :]
            behind = cot2_h[side, spot, :]
            ours = cot1_o[side, spot, :]
            swum = swim * adjoint
            spread_out = halo_row(side, KAPPA, 0, layer) * adjoint
            drift = halo_row(side, EAST, 0, layer) * swum
            outer_coef = halo_row(side, KAPPA, 1, layer) - sign * swim * halo_row(side, NORTH, 1, layer)
            inner_coef = spread(field[KAPPA, layer, inner(side), :]) + sign * swim * spread(
                field[NORTH, layer, inner(side), :]
            )
            pull = (
                halo_row(side, CENTRE, 0, layer) * adjoint
                + rolled(spread_out - drift, 1, 1)
                + rolled(spread_out + drift, -1, 1)
                + outer_coef * behind
                + inner_coef * ours
            )
            alive = survival_h(side, 1, first, layer)
            kept_h[side, spot, :] = pull * alive
            added = inflow[side, spot, :] * alive
            west_val = rolled(added, 1, 1)
            east_val = rolled(added, -1, 1)
            wet = wet_edge[side, spot, :]
            beyond[1, side, layer] -= wide(1, first) * (pull * added)
            edge_sum[side, KAPPA_NEAR, layer] += adjoint * (wet + (west_val + east_val) - 4.0 * added)
            edge_sum[side, NORTH_NEAR, layer] += swum * wet
            edge_sum[side, EAST_NEAR, layer] += swum * (east_val - west_val)
            edge_sum[side, KAPPA_FAR, layer] += behind * added
            edge_sum[side, NORTH_FAR, layer] += swim * (behind * added)
            edge_sum[side, KAPPA_OWN, layer] += ours * added
            edge_sum[side, NORTH_OWN, layer] += swim * (ours * added)

    over_groups(back2_halo)
    for side in range(2):
        for layer in range(layers):
            spot = side * layers + layer
            beyond_o[spot : spot + 1, :] = column(beyond[1, side, layer])
    beyonds = [
        pltpu.make_async_remote_copy(
            src_ref=beyond_o,
            dst_ref=beyond_in.at[by],
            send_sem=coh_send.at[2 * STEPS, by],
            recv_sem=coh_recv.at[2 * STEPS, by],
            device_id={"coh": peer},
            device_id_type=MESH,
        )
        for by, peer in enumerate(peers)
    ]
    for copy in beyonds:
        copy.start()

    summed(2)
    for copy in beyonds:
        copy.wait_recv()
    outside = beyond_o[...]
    for by in range(n_coh - 1):
        outside = outside + beyond_in[by]
    outside = outside * (1.0 / every)
    for side in range(2):
        for layer in range(layers):
            press_o[side, layer : layer + 1] = total[2, layer, inner(side), :]
        press_o[side, layers : 2 * layers] = outside[side * layers : (side + 1) * layers]
    send(PRESS2)
    receive(PRESS2)
    for layer in range(layers):
        spot = slice(layers + layer, layers + layer + 1)
        total[2, layer] += jnp.where(is_first, press_h[0, spot, :], 0.0) + jnp.where(
            is_last, press_h[1, spot, :], 0.0
        )

    def inflow_first(first, layer, spot):
        swim = wide(3, first)
        for side in range(2):
            here = slice(side * layers + layer, side * layers + layer + 1)
            pressure = press_h[side, layer : layer + 1, :] + outside[here]
            adjoint = kept_h[side, spot, :] + wide(2, first) * spread(pressure)
            into[side, spot, :] = coefs[side, spot, :] * adjoint
            product = adjoint * wet1_edge[side, spot, :]
            edge_sum[side, KAPPA_NEAR, layer] += product
            edge_sum[side, NORTH_NEAR, layer] += swim * product

    over_groups(inflow_first)
    for side in range(2):
        for index in range(SENT):
            for layer in range(layers):
                spot = index * layers + layer
                edge_o[side, spot : spot + 1] = column(edge_sum[side, index, layer])
    send(EDGE)

    def back1(cohort, sums):
        mortal, crowding, weight, swim = scalars(cohort)
        added = []
        for layer in range(layers):
            spot = pl.ds(layer * cohorts + cohort, 1)
            adjoint = kept[cohort, layer] + weight * total[2, layer]
            swum = swim * adjoint
            grads[0, layer] += swum * east1[cohort, layer]
            grads[1, layer] += swum * north1[cohort, layer]
            grads[2, layer] += adjoint * lap1[cohort, layer]
            pull = pulled(adjoint, swum, layer, (into[0, spot, :], into[1, spot, :]))
            last[cohort, layer] = pull * surv1[cohort, layer]
            added.append(sums[layer] - crowding * (pull * wet1[cohort, layer]))
        return tuple(added)

    sums = lax.fori_loop(0, cohorts, back1, (zero,) * layers)
    for layer in range(layers):
        partial[3, layer] = sums[layer]
    for copy in exchange(3):
        copy.start()

    put = pltpu.make_async_copy(last, out, local_sem.at[2])
    put.start()

    receive(EDGE)
    part = lon // n_coh
    for layer in range(layers):
        ocean = field[OCEAN, layer]
        near = (is_first, is_last)
        behind = (row == 1, row == rows - 2)
        drift, climb, kappa = (grads[index, layer] for index in range(3))
        for side in range(2):

            def got(index):
                spot = index * layers + layer
                return edge_h[side, spot : spot + 1, :]

            sign = -1.0 if side == 0 else 1.0
            kappa_near = got(KAPPA_NEAR) + column(edge_sum[side, KAPPA_OWN, layer])
            north_near = sign * (got(NORTH_NEAR) + column(edge_sum[side, NORTH_OWN, layer]))
            drift = drift + jnp.where(near[side], got(EAST_NEAR), 0.0)
            climb = climb + jnp.where(near[side], north_near, 0.0)
            climb = climb + jnp.where(behind[side], sign * got(NORTH_FAR), 0.0)
            kappa = kappa + jnp.where(near[side], kappa_near, 0.0)
            kappa = kappa + jnp.where(behind[side], got(KAPPA_FAR), 0.0)
        values = (-0.5 * ocean * drift, -0.5 * ocean * climb, ocean * kappa)
        for index, value in enumerate(values):
            for to in range(n_coh):
                share[to, index, layer] = value[:, to * part : (to + 1) * part]
    shares = [
        pltpu.make_async_remote_copy(
            src_ref=share.at[peer],
            dst_ref=share_in.at[by],
            send_sem=share_send.at[by],
            recv_sem=share_recv.at[by],
            device_id={"coh": peer},
            device_id_type=MESH,
        )
        for by, peer in enumerate(peers)
    ]
    for copy in shares:
        copy.start()

    summed(3)
    out_press[...] = total[3]
    for copy in shares:
        copy.wait_recv()
    for index in range(3):
        value = share[coh, index]
        for by in range(n_coh - 1):
            value = value + share_in[by, index]
        out_grads[index] = value

    put.wait()
    for kind in messages:
        sent(kind)
    for which in range(2 * STEPS):
        for copy in exchange(which):
            copy.wait_send()
    for copy in shares + beyonds:
        copy.wait_send()


def finish(age, mass, last, press, grads, out, out_east, out_north, out_kappa):
    group, layers = out.shape[0], out.shape[1]
    step = pl.program_id(0)
    for cohort in range(group):
        weight = mass[age[step * group + cohort]]
        for layer in range(layers):
            out[cohort, layer] = last[cohort, layer] + weight * press[layer]

    @pl.when(step == 0)
    def _():
        for index, target in enumerate((out_east, out_north, out_kappa)):
            target[...] = grads[index]


def local(*args):
    density = args[0]
    cohorts, layers, rows, lon = density.shape
    n_lat, n_coh = lax.axis_size("lat"), lax.axis_size("coh")
    f32 = jnp.float32
    vmem = pl.BlockSpec(memory_space=pltpu.VMEM)
    smem = pl.BlockSpec(memory_space=pltpu.SMEM)
    share = jax.ShapeDtypeStruct((layers, rows, lon // n_coh), f32)
    whole = pltpu.VMEM(density.shape, f32)
    packed = pltpu.VMEM((2, layers * cohorts, lon), f32)
    def vec(*shape):
        return pltpu.VMEM(shape, f32)

    part = lon // n_coh
    hbm = pl.BlockSpec(memory_space=pl.ANY)
    scratch = [
        whole,
        whole,
        whole,
        vec(5, layers, rows, lon),
        vec(2, 5, 2 * layers, lon),
        vec(4, cohorts, 128),
        whole,
        whole,
        whole,
        whole,
        whole,
        whole,
        whole,
        vec(4, layers, rows, lon),
        vec(4, layers, rows, lon),
        vec(4, n_coh - 1, layers, rows, lon),
        vec(3, layers, rows, lon),
        vec(n_coh, 3, layers, rows, part),
        vec(n_coh - 1, 3, layers, rows, part),
        packed,
        vec(2, 4, 2 * layers, lon),
        vec(2, 4, 2 * layers, lon),
        packed,
        packed,
        packed,
        packed,
        vec(2, 2, layers, lon),
        vec(2, 2, layers, lon),
        vec(2, 2 * layers, lon),
        vec(2, 2 * layers, lon),
        vec(2, SENT * layers, lon),
        vec(2, SENT * layers, lon),
        vec(2, 7, layers, 8, lon),
        vec(2, 2, layers, 8, lon),
        vec(2 * layers, lon),
        vec(n_coh - 1, 2 * layers, lon),
        packed,
        packed,
        packed,
        packed,
        packed,
        packed,
        pltpu.SemaphoreType.DMA((3,)),
        pltpu.SemaphoreType.DMA((7, 2)),
        pltpu.SemaphoreType.DMA((7, 2)),
        pltpu.SemaphoreType.DMA((5, n_coh - 1)),
        pltpu.SemaphoreType.DMA((5, n_coh - 1)),
        pltpu.SemaphoreType.DMA((n_coh - 1,)),
        pltpu.SemaphoreType.DMA((n_coh - 1,)),
    ]
    size = density.size
    last, press, grads = pl.pallas_call(
        functools.partial(kernel, n_lat, n_coh),
        out_shape=(
            jax.ShapeDtypeStruct(density.shape, f32),
            jax.ShapeDtypeStruct((layers, rows, lon), f32),
            jax.ShapeDtypeStruct((3, layers, rows, part), f32),
        ),
        in_specs=[hbm] * 2 + [vmem] * 4 + [smem] * 5,
        out_specs=(hbm, vmem, vmem),
        scratch_shapes=scratch,
        compiler_params=pltpu.CompilerParams(
            collective_id=0, has_side_effects=True, vmem_limit_bytes=56 * 1024 * 1024
        ),
        cost_estimate=pl.CostEstimate(
            flops=150 * size, bytes_accessed=12 * size, transcendentals=2 * size
        ),
    )(*args)
    group = max(1, cohorts // 8)
    block = pl.BlockSpec((group, layers, rows, lon), lambda step: (step, 0, 0, 0))
    return pl.pallas_call(
        finish,
        grid=(cohorts // group,),
        out_shape=(jax.ShapeDtypeStruct(density.shape, f32), share, share, share),
        in_specs=[smem, smem, block, vmem, vmem],
        out_specs=(block, vmem, vmem, vmem),
        compiler_params=pltpu.CompilerParams(vmem_limit_bytes=56 * 1024 * 1024),
        cost_estimate=pl.CostEstimate(flops=2 * size, bytes_accessed=8 * size, transcendentals=0),
    )(args[6], args[9], last, press, grads)


def solution(mesh):
    fields = P(None, "lat", None)
    in_specs = (P("coh", None, "lat", None),) * 2 + (fields,) * 4 + (P("coh"),) + (P(),) * 4
    out_specs = (P("coh", None, "lat", None),) + (P(None, "lat", "coh"),) * 3
    return jax.shard_map(local, mesh=mesh, in_specs=in_specs, out_specs=out_specs, check_vma=False)
```

```python
import functools

import jax
import jax.numpy as jnp
from jax import lax
from jax.experimental import pallas as pl
from jax.experimental.pallas import tpu as pltpu
from jax.sharding import PartitionSpec as P

STEPS = 2
MESH = pl.DeviceIdType.MESH
FIELDS, COT1, COT2, PART2, CROWD2, PRESS2, EDGE = range(7)
KAPPA_NEAR, NORTH_NEAR, EAST_NEAR, KAPPA_FAR, NORTH_FAR, KAPPA_OWN, NORTH_OWN = range(7)
SENT = 5
GROUP = 4
CHUNKS = 8
CENTRE, KAPPA, EAST, NORTH, OCEAN = range(5)


def rolled(value, by, axis):
    return pltpu.roll(value, by % value.shape[axis], axis)


def kernel(
    n_lat,
    n_coh,
    dens_in,
    cot_in,
    land,
    east,
    north,
    diff,
    age,
    mort,
    crowd_coef,
    mass,
    speed,
    out,
    out_press,
    out_grads,
    dens,
    cot,
    last,
    field,
    halo_field,
    params,
    state,
    surv1,
    wet1,
    lap1,
    east1,
    north1,
    kept,
    total,
    partial,
    arrived,
    grads,
    share,
    share_in,
    dens_edge,
    field_o,
    field_h,
    cot1_o,
    cot1_h,
    cot2_o,
    cot2_h,
    part_o,
    part_h,
    crowd_o,
    crowd_h,
    press_o,
    press_h,
    edge_o,
    edge_h,
    edge_sum,
    beyond,
    beyond_o,
    beyond_in,
    outside,
    wet_edge,
    wet1_edge,
    coefs,
    inflow,
    into,
    kept_h,
    local_sem,
    lat_send,
    lat_recv,
    coh_send,
    coh_recv,
):
    cohorts, layers, rows, lon = dens.shape
    chunk = cohorts // CHUNKS

    def fetch(source, target, which):
        return [
            pltpu.make_async_copy(
                source.at[pl.ds(at * chunk, chunk)],
                target.at[pl.ds(at * chunk, chunk)],
                local_sem.at[which, at],
            )
            for at in range(CHUNKS)
        ]

    get_dens = fetch(dens_in, dens, 0)
    get_cot = fetch(cot_in, cot, 1)
    for copy in get_dens + get_cot:
        copy.start()
    every = cohorts * n_coh
    lat = lax.axis_index("lat")
    coh = lax.axis_index("coh")
    has_low = lat > 0
    has_high = lat < n_lat - 1
    low = jnp.maximum(lat - 1, 0)
    high = jnp.minimum(lat + 1, n_lat - 1)
    peers = [lax.rem(coh + by, n_coh) for by in range(1, n_coh)]

    barrier = pltpu.get_barrier_semaphore()
    for peer in peers:
        pl.semaphore_signal(barrier, inc=1, device_id={"coh": peer}, device_id_type=MESH)

    @pl.when(has_low)
    def _():
        pl.semaphore_signal(barrier, inc=1, device_id={"lat": low}, device_id_type=MESH)

    @pl.when(has_high)
    def _():
        pl.semaphore_signal(barrier, inc=1, device_id={"lat": high}, device_id_type=MESH)

    buffers = {
        FIELDS: (field_o, field_h),
        COT1: (cot1_o, cot1_h),
        COT2: (cot2_o, cot2_h),
        PART2: (part_o, part_h),
        CROWD2: (crowd_o, crowd_h),
        PRESS2: (press_o, press_h),
        EDGE: (edge_o, edge_h),
    }

    def message(kind, layer):
        outgoing, incoming = buffers[kind]

        def one(side, device):
            return pltpu.make_async_remote_copy(
                src_ref=outgoing.at[side, layer],
                dst_ref=incoming.at[1 - side, layer],
                send_sem=lat_send.at[kind, layer, side],
                recv_sem=lat_recv.at[kind, layer, 1 - side],
                device_id={"lat": device},
                device_id_type=MESH,
            )

        return one(0, low), one(1, high)

    def send(kind, layer):
        to_low, to_high = message(kind, layer)

        @pl.when(has_low)
        def _():
            to_low.start()

        @pl.when(has_high)
        def _():
            to_high.start()

    def receive(kind, layer):
        to_low, to_high = message(kind, layer)

        @pl.when(has_low)
        def _():
            to_high.wait_recv()

        @pl.when(has_high)
        def _():
            to_low.wait_recv()

    def sent(kind, layer):
        to_low, to_high = message(kind, layer)

        @pl.when(has_low)
        def _():
            to_low.wait_send()

        @pl.when(has_high)
        def _():
            to_high.wait_send()

    def to_peers(kind, layer, source, target):
        return [
            pltpu.make_async_remote_copy(
                src_ref=source(peer),
                dst_ref=target(by),
                send_sem=coh_send.at[kind, layer, by],
                recv_sem=coh_recv.at[kind, layer, by],
                device_id={"coh": peer},
                device_id_type=MESH,
            )
            for by, peer in enumerate(peers)
        ]

    def exchange(which, layer):
        return to_peers(
            which,
            layer,
            lambda peer: partial.at[which, layer],
            lambda by: arrived.at[which, by, layer],
        )

    def exchange_beyond(layer):
        return to_peers(
            2 * STEPS, layer, lambda peer: beyond_o.at[layer], lambda by: beyond_in.at[by, layer]
        )

    def exchange_share(layer):
        return to_peers(
            2 * STEPS + 1,
            layer,
            lambda peer: share.at[peer, layer],
            lambda by: share_in.at[by, layer],
        )

    def begin(copies):
        for copy in copies:
            copy.start()

    def summed(which, layer):
        for copy in exchange(which, layer):
            copy.wait_recv()
        value = partial[which, layer]
        for by in range(n_coh - 1):
            value = value + arrived[which, by, layer]
        total[which, layer] = value * (1.0 / every)

    def pack(source, layer, low_row, high_row, target):
        def body(step, carry):
            for member in range(GROUP):
                cohort = step * GROUP + member
                spot = pl.ds(cohort, 1)
                target[0, layer, spot, :] = source[cohort, layer, low_row : low_row + 1, :]
                target[1, layer, spot, :] = source[cohort, layer, high_row : high_row + 1, :]
            return carry

        lax.fori_loop(0, cohorts // GROUP, body, 0)

    for layer in range(layers):
        raw = (land[layer].astype(jnp.float32), east[layer], north[layer], diff[layer])
        for index, value in enumerate(raw):
            for depth in range(2):
                spot = slice(2 * index + depth, 2 * index + depth + 1)
                field_o[0, layer, spot, :] = value[depth : depth + 1]
                field_o[1, layer, spot, :] = value[rows - 1 - depth : rows - depth]

    for side, exists in ((0, has_low), (1, has_high)):

        @pl.when(jnp.logical_not(exists))
        def _(side=side):
            for _, target in buffers.values():
                target[side] = jnp.zeros(target.shape[1:], jnp.float32)

    pl.semaphore_wait(
        barrier, n_coh - 1 + has_low.astype(jnp.int32) + has_high.astype(jnp.int32)
    )
    for layer in range(layers):
        send(FIELDS, layer)
    for copy in get_dens:
        copy.wait()

    zero = jnp.zeros((rows, lon), jnp.float32)

    def over_cohorts(body):
        def one(step, carry):
            return body([step * GROUP + member for member in range(GROUP)], carry)

        return lax.fori_loop(0, cohorts // GROUP, one, zero)

    def added_up(values):
        value = values[0]
        for other in values[1:]:
            value = value + other
        return value

    for layer in range(layers):

        def weigh(group, sums, layer=layer):
            return sums + added_up([mass[age[cohort]] * dens[cohort, layer] for cohort in group])

        partial[0, layer] = over_cohorts(weigh)
        begin(exchange(0, layer))

    for layer in range(layers):
        ocean = land[layer].astype(jnp.float32)
        kappa = diff[layer]
        field[CENTRE, layer] = ocean * (1.0 - 4.0 * kappa)
        field[KAPPA, layer] = ocean * kappa
        field[EAST, layer] = ocean * (0.5 * east[layer])
        field[NORTH, layer] = ocean * (0.5 * north[layer])
        field[OCEAN, layer] = ocean
    for cohort in range(cohorts):
        one = age[cohort]
        for index, table in enumerate((mort, crowd_coef, mass, speed)):
            params[index, cohort : cohort + 1, :] = jnp.full((1, 128), table[one], jnp.float32)
    for copy in get_cot:
        copy.wait()
    for layer in range(layers):
        pack(cot, layer, 0, rows - 1, cot1_o)
        send(COT1, layer)
    for layer in range(layers):
        pack(cot, layer, 1, rows - 2, cot2_o)
        send(COT2, layer)
    for layer in range(layers):
        pack(dens, layer, 0, rows - 1, dens_edge)
    grads[...] = jnp.zeros(grads.shape, jnp.float32)
    edge_sum[...] = jnp.zeros(edge_sum.shape, jnp.float32)
    beyond[...] = jnp.zeros(beyond.shape, jnp.float32)

    def wide(index, first):
        value = params[index, pl.ds(first, 8), :]
        return jnp.concatenate([value] * (lon // 128), axis=1)

    def spread(row):
        return jnp.broadcast_to(row, (8, lon))

    def over_groups(body):
        def one(group, carry):
            first = pl.multiple_of(group * 8, 8)
            body(first, pl.ds(first, 8))
            return carry

        lax.fori_loop(0, cohorts // 8, one, 0)

    def halo_row(side, index, depth, layer):
        return spread(halo_field[side, layer, 2 * index + depth : 2 * index + depth + 1, :])

    for layer in range(layers):
        receive(FIELDS, layer)
        for side in range(2):
            raw = [field_h[side, layer, 2 * index : 2 * index + 2] for index in range(4)]
            ocean, kappa = raw[0], raw[3]
            values = (
                ocean * (1.0 - 4.0 * kappa),
                ocean * kappa,
                ocean * (0.5 * raw[1]),
                ocean * (0.5 * raw[2]),
                ocean,
            )
            for index, value in enumerate(values):
                halo_field[side, layer, 2 * index : 2 * index + 2] = value

    def survival_h(side, first, layer):
        crowd = spread(crowd_h[side, layer])
        return halo_row(side, OCEAN, 0, layer) * jnp.exp(-(wide(0, first) + wide(1, first) * crowd))

    def inner(side):
        return slice(0, 1) if side == 0 else slice(rows - 1, rows)

    def column(value):
        return jnp.sum(value, axis=0, keepdims=True)

    row = lax.broadcasted_iota(jnp.int32, (rows, lon), 0)
    is_first = row == 0
    is_last = row == rows - 1

    def from_before(value, edge):
        return jnp.where(is_first, edge, rolled(value, 1, 0))

    def from_after(value, edge):
        return jnp.where(is_last, edge, rolled(value, -1, 0))

    def scalars(cohort):
        one = age[cohort]
        return mort[one], crowd_coef[one], mass[one], speed[one]

    def survival(layer, which, mortal, crowding):
        return field[OCEAN, layer] * jnp.exp(-(mortal + crowding * total[which, layer]))

    def first_step(layer):
        summed(0, layer)

        def outflow(first, spot):
            swim = wide(3, first)
            for side in range(2):
                crowd = spread(total[0, layer, inner(side), :])
                ocean = spread(field[OCEAN, layer, inner(side), :])
                alive = ocean * jnp.exp(-(wide(0, first) + wide(1, first) * crowd))
                wet = dens_edge[side, layer, spot, :] * alive
                shift = swim * halo_row(side, NORTH, 0, layer)
                kappa = halo_row(side, KAPPA, 0, layer)
                coef = kappa - shift if side == 0 else kappa + shift
                value = coef * wet
                wet1_edge[side, layer, spot, :] = wet
                coefs[side, layer, spot, :] = coef
                inflow[side, layer, spot, :] = value
                beyond[0, side, layer] += wide(2, first) * value

        over_groups(outflow)
        for side in range(2):
            part_o[side, layer] = column(beyond[0, side, layer])
        send(PART2, layer)

        def forward(group, sums):
            added = []
            for cohort in group:
                mortal, crowding, weight, swim = scalars(cohort)
                alive = survival(layer, 0, mortal, crowding)
                wet = dens[cohort, layer] * alive
                before = from_before(wet, 0.0)
                after = from_after(wet, 0.0)
                west_val = rolled(wet, 1, 1)
                east_val = rolled(wet, -1, 1)
                around = (before + after) + (west_val + east_val)
                east_diff = east_val - west_val
                north_diff = after - before
                value = (
                    field[CENTRE, layer] * wet
                    + field[KAPPA, layer] * around
                    - swim * (field[EAST, layer] * east_diff + field[NORTH, layer] * north_diff)
                )
                surv1[cohort, layer] = alive
                wet1[cohort, layer] = wet
                lap1[cohort, layer] = around - 4.0 * wet
                east1[cohort, layer] = east_diff
                north1[cohort, layer] = north_diff
                state[cohort, layer] = value
                added.append(weight * value)
            return sums + added_up(added)

        sums = over_cohorts(forward)
        receive(PART2, layer)
        partial[1, layer] = sums + (
            jnp.where(is_first, part_h[0, layer], 0.0) + jnp.where(is_last, part_h[1, layer], 0.0)
        )
        begin(exchange(1, layer))

    def pulled(adjoint, swum, layer, spot):
        spread_out = field[KAPPA, layer] * adjoint
        drift = field[EAST, layer] * swum
        climb = field[NORTH, layer] * swum
        return (
            field[CENTRE, layer] * adjoint
            + rolled(spread_out - drift, 1, 1)
            + rolled(spread_out + drift, -1, 1)
            + from_before(spread_out - climb, into[0, layer, spot, :])
            + from_after(spread_out + climb, into[1, layer, spot, :])
        )

    def second_back(layer):
        receive(COT1, layer)

        def inflow_cot(first, spot):
            for side in range(2):
                into[side, layer, spot, :] = coefs[side, layer, spot, :] * cot1_h[side, layer, spot, :]

        over_groups(inflow_cot)
        summed(1, layer)
        for side in range(2):
            crowd_o[side, layer] = total[1, layer, inner(side), :]
        send(CROWD2, layer)

        def back2(group, sums):
            added = []
            products = []
            for cohort in group:
                mortal, crowding, weight, swim = scalars(cohort)
                spot = pl.ds(cohort, 1)
                alive = survival(layer, 1, mortal, crowding)
                wet = state[cohort, layer] * alive
                wet_edge[0, layer, spot, :] = wet[:1]
                wet_edge[1, layer, spot, :] = wet[rows - 1 :]
                before = from_before(wet, 0.0)
                after = from_after(wet, 0.0)
                west_val = rolled(wet, 1, 1)
                east_val = rolled(wet, -1, 1)
                adjoint = cot[cohort, layer]
                swum = swim * adjoint
                products.append(
                    (
                        swum * (east_val - west_val),
                        swum * (after - before),
                        adjoint * ((before + after) + (west_val + east_val) - 4.0 * wet),
                    )
                )
                pull = pulled(adjoint, swum, layer, spot)
                kept[cohort, layer] = pull * alive
                added.append(crowding * (pull * wet))
            for index in range(3):
                grads[index, layer] += added_up([product[index] for product in products])
            return sums - added_up(added)

        partial[2, layer] = over_cohorts(back2)
        begin(exchange(2, layer))

    def second_beyond(layer):
        receive(CROWD2, layer)
        receive(COT2, layer)

        def back2_halo(first, spot):
            swim = wide(3, first)
            for side in range(2):
                sign = 1.0 if side == 0 else -1.0
                adjoint = cot1_h[side, layer, spot, :]
                behind = cot2_h[side, layer, spot, :]
                ours = cot1_o[side, layer, spot, :]
                swum = swim * adjoint
                spread_out = halo_row(side, KAPPA, 0, layer) * adjoint
                drift = halo_row(side, EAST, 0, layer) * swum
                outer_coef = halo_row(side, KAPPA, 1, layer) - sign * swim * halo_row(side, NORTH, 1, layer)
                inner_coef = spread(field[KAPPA, layer, inner(side), :]) + sign * swim * spread(
                    field[NORTH, layer, inner(side), :]
                )
                pull = (
                    halo_row(side, CENTRE, 0, layer) * adjoint
                    + rolled(spread_out - drift, 1, 1)
                    + rolled(spread_out + drift, -1, 1)
                    + outer_coef * behind
                    + inner_coef * ours
                )
                alive = survival_h(side, first, layer)
                kept_h[side, layer, spot, :] = pull * alive
                added = inflow[side, layer, spot, :] * alive
                west_val = rolled(added, 1, 1)
                east_val = rolled(added, -1, 1)
                wet = wet_edge[side, layer, spot, :]
                beyond[1, side, layer] -= wide(1, first) * (pull * added)
                edge_sum[side, KAPPA_NEAR, layer] += adjoint * (wet + (west_val + east_val) - 4.0 * added)
                edge_sum[side, NORTH_NEAR, layer] += swum * wet
                edge_sum[side, EAST_NEAR, layer] += swum * (east_val - west_val)
                edge_sum[side, KAPPA_FAR, layer] += behind * added
                edge_sum[side, NORTH_FAR, layer] += swim * (behind * added)
                edge_sum[side, KAPPA_OWN, layer] += ours * added
                edge_sum[side, NORTH_OWN, layer] += swim * (ours * added)

        over_groups(back2_halo)
        for side in range(2):
            beyond_o[layer, side : side + 1, :] = column(beyond[1, side, layer])
        begin(exchange_beyond(layer))

    def second_pressure(layer):
        summed(2, layer)
        for copy in exchange_beyond(layer):
            copy.wait_recv()
        value = beyond_o[layer]
        for by in range(n_coh - 1):
            value = value + beyond_in[by, layer]
        value = value * (1.0 / every)
        outside[layer] = value
        for side in range(2):
            press_o[side, layer, :1] = total[2, layer, inner(side), :]
            press_o[side, layer, 1:] = value[side : side + 1]
        send(PRESS2, layer)

    def first_back(layer):
        receive(PRESS2, layer)
        total[2, layer] += jnp.where(is_first, press_h[0, layer, 1:], 0.0) + jnp.where(
            is_last, press_h[1, layer, 1:], 0.0
        )

        def inflow_first(first, spot):
            swim = wide(3, first)
            for side in range(2):
                pressure = press_h[side, layer, :1] + outside[layer, side : side + 1]
                adjoint = kept_h[side, layer, spot, :] + wide(2, first) * spread(pressure)
                into[side, layer, spot, :] = coefs[side, layer, spot, :] * adjoint
                product = adjoint * wet1_edge[side, layer, spot, :]
                edge_sum[side, KAPPA_NEAR, layer] += product
                edge_sum[side, NORTH_NEAR, layer] += swim * product

        over_groups(inflow_first)
        for side in range(2):
            for index in range(SENT):
                edge_o[side, layer, index : index + 1] = column(edge_sum[side, index, layer])
        send(EDGE, layer)

        def back1(group, sums):
            added = []
            products = []
            for cohort in group:
                mortal, crowding, weight, swim = scalars(cohort)
                adjoint = kept[cohort, layer] + weight * total[2, layer]
                swum = swim * adjoint
                products.append(
                    (
                        swum * east1[cohort, layer],
                        swum * north1[cohort, layer],
                        adjoint * lap1[cohort, layer],
                    )
                )
                pull = pulled(adjoint, swum, layer, pl.ds(cohort, 1))
                last[cohort, layer] = pull * surv1[cohort, layer]
                added.append(crowding * (pull * wet1[cohort, layer]))
            for index in range(3):
                grads[index, layer] += added_up([product[index] for product in products])
            return sums - added_up(added)

        partial[3, layer] = over_cohorts(back1)
        begin(exchange(3, layer))

    def put(layer):
        return [
            pltpu.make_async_copy(
                last.at[pl.ds(at * chunk, chunk), layer],
                out.at[pl.ds(at * chunk, chunk), layer],
                local_sem.at[2 + layer, at],
            )
            for at in range(CHUNKS)
        ]

    part = lon // n_coh

    def gradients(layer):
        receive(EDGE, layer)
        ocean = field[OCEAN, layer]
        near = (is_first, is_last)
        behind = (row == 1, row == rows - 2)
        drift, climb, kappa = (grads[index, layer] for index in range(3))
        for side in range(2):

            def got(index):
                return edge_h[side, layer, index : index + 1, :]

            sign = -1.0 if side == 0 else 1.0
            kappa_near = got(KAPPA_NEAR) + column(edge_sum[side, KAPPA_OWN, layer])
            north_near = sign * (got(NORTH_NEAR) + column(edge_sum[side, NORTH_OWN, layer]))
            drift = drift + jnp.where(near[side], got(EAST_NEAR), 0.0)
            climb = climb + jnp.where(near[side], north_near, 0.0)
            climb = climb + jnp.where(behind[side], sign * got(NORTH_FAR), 0.0)
            kappa = kappa + jnp.where(near[side], kappa_near, 0.0)
            kappa = kappa + jnp.where(behind[side], got(KAPPA_FAR), 0.0)
        values = (-0.5 * ocean * drift, -0.5 * ocean * climb, ocean * kappa)
        for index, value in enumerate(values):
            for to in range(n_coh):
                share[to, layer, index] = value[:, to * part : (to + 1) * part]
        begin(exchange_share(layer))

    for layer in range(layers):
        first_step(layer)
    for layer in range(layers):
        second_back(layer)
        if layer > 0:
            second_pressure(layer - 1)
        second_beyond(layer)
    for layer in range(layers):
        if layer == layers - 1:
            second_pressure(layer)
        if layer > 0:
            gradients(layer - 1)
        first_back(layer)
        begin(put(layer))
    gradients(layers - 1)
    for layer in range(layers):
        summed(3, layer)
        out_press[layer] = total[3, layer]
        for copy in exchange_share(layer):
            copy.wait_recv()
        for index in range(3):
            value = share[coh, layer, index]
            for by in range(n_coh - 1):
                value = value + share_in[by, layer, index]
            out_grads[index, layer] = value

    for layer in range(layers):
        for copy in put(layer):
            copy.wait()
        for kind in buffers:
            sent(kind, layer)
        for which in range(2 * STEPS):
            for copy in exchange(which, layer):
                copy.wait_send()
        for copy in exchange_beyond(layer) + exchange_share(layer):
            copy.wait_send()


def finish(age, mass, last, press, grads, out, out_east, out_north, out_kappa, held, sem):
    cohorts, layers = held.shape[:2]
    chunk = cohorts // CHUNKS
    spots = [pl.ds(at * chunk, chunk) for at in range(CHUNKS)]
    get = [
        pltpu.make_async_copy(last.at[spot], held.at[spot], sem.at[0, at])
        for at, spot in enumerate(spots)
    ]
    put = [
        pltpu.make_async_copy(held.at[spot], out.at[spot], sem.at[1, at])
        for at, spot in enumerate(spots)
    ]
    for copy in get:
        copy.start()
    for index, target in enumerate((out_east, out_north, out_kappa)):
        target[...] = grads[index]
    for at in range(CHUNKS):
        get[at].wait()
        for cohort in range(at * chunk, (at + 1) * chunk):
            weight = mass[age[cohort]]
            for layer in range(layers):
                held[cohort, layer] += weight * press[layer]
        put[at].start()
    for copy in put:
        copy.wait()


def local(*args):
    density = args[0]
    cohorts, layers, rows, lon = density.shape
    n_lat, n_coh = lax.axis_size("lat"), lax.axis_size("coh")
    f32 = jnp.float32
    vmem = pl.BlockSpec(memory_space=pltpu.VMEM)
    smem = pl.BlockSpec(memory_space=pltpu.SMEM)
    share = jax.ShapeDtypeStruct((layers, rows, lon // n_coh), f32)
    whole = pltpu.VMEM(density.shape, f32)
    packed = pltpu.VMEM((2, layers, cohorts, lon), f32)
    def vec(*shape):
        return pltpu.VMEM(shape, f32)

    part = lon // n_coh
    hbm = pl.BlockSpec(memory_space=pl.ANY)
    scratch = (
        [whole] * 3
        + [
            vec(5, layers, rows, lon),
            vec(2, layers, 10, lon),
            vec(4, cohorts, 128),
        ]
        + [whole] * 7
        + [
            vec(4, layers, rows, lon),
            vec(4, layers, rows, lon),
            vec(4, n_coh - 1, layers, rows, lon),
            vec(3, layers, rows, lon),
            vec(n_coh, layers, 3, rows, part),
            vec(n_coh - 1, layers, 3, rows, part),
            packed,
            vec(2, layers, 8, lon),
            vec(2, layers, 8, lon),
            packed,
            packed,
            packed,
            packed,
            vec(2, layers, 1, lon),
            vec(2, layers, 1, lon),
            vec(2, layers, 1, lon),
            vec(2, layers, 1, lon),
            vec(2, layers, 2, lon),
            vec(2, layers, 2, lon),
            vec(2, layers, SENT, lon),
            vec(2, layers, SENT, lon),
            vec(2, 7, layers, 8, lon),
            vec(2, 2, layers, 8, lon),
            vec(layers, 2, lon),
            vec(n_coh - 1, layers, 2, lon),
            vec(layers, 2, lon),
        ]
        + [packed] * 6
        + [
            pltpu.SemaphoreType.DMA((2 + layers, CHUNKS)),
            pltpu.SemaphoreType.DMA((7, layers, 2)),
            pltpu.SemaphoreType.DMA((7, layers, 2)),
            pltpu.SemaphoreType.DMA((6, layers, n_coh - 1)),
            pltpu.SemaphoreType.DMA((6, layers, n_coh - 1)),
        ]
    )
    size = density.size
    last, press, grads = pl.pallas_call(
        functools.partial(kernel, n_lat, n_coh),
        out_shape=(
            jax.ShapeDtypeStruct(density.shape, f32),
            jax.ShapeDtypeStruct((layers, rows, lon), f32),
            jax.ShapeDtypeStruct((3, layers, rows, part), f32),
        ),
        in_specs=[hbm] * 2 + [vmem] * 4 + [smem] * 5,
        out_specs=(hbm, vmem, vmem),
        scratch_shapes=scratch,
        compiler_params=pltpu.CompilerParams(
            collective_id=0, has_side_effects=True, vmem_limit_bytes=56 * 1024 * 1024
        ),
        cost_estimate=pl.CostEstimate(
            flops=150 * size, bytes_accessed=12 * size, transcendentals=2 * size
        ),
    )(*args)
    return pl.pallas_call(
        finish,
        out_shape=(jax.ShapeDtypeStruct(density.shape, f32), share, share, share),
        in_specs=[smem, smem, hbm, vmem, vmem],
        out_specs=(hbm, vmem, vmem, vmem),
        scratch_shapes=[whole, pltpu.SemaphoreType.DMA((2, CHUNKS))],
        compiler_params=pltpu.CompilerParams(vmem_limit_bytes=56 * 1024 * 1024),
        cost_estimate=pl.CostEstimate(flops=2 * size, bytes_accessed=8 * size, transcendentals=0),
    )(args[6], args[9], last, press, grads)


def solution(mesh):
    fields = P(None, "lat", None)
    in_specs = (P("coh", None, "lat", None),) * 2 + (fields,) * 4 + (P("coh"),) + (P(),) * 4
    out_specs = (P("coh", None, "lat", None),) + (P(None, "lat", "coh"),) * 3
    return jax.shard_map(local, mesh=mesh, in_specs=in_specs, out_specs=out_specs, check_vma=False)
```

```python
import functools

import jax
import jax.numpy as jnp
from jax import lax
from jax.experimental import pallas as pl
from jax.experimental.pallas import tpu as pltpu
from jax.sharding import PartitionSpec as P

STEPS = 2
MESH = pl.DeviceIdType.MESH
FIELDS, COT1, COT2, PART2, CROWD2, PRESS2, EDGE = range(7)
KAPPA_NEAR, NORTH_NEAR, EAST_NEAR, KAPPA_FAR, NORTH_FAR, KAPPA_OWN, NORTH_OWN = range(7)
SENT = 5
GROUP = 16
LANES = 128
CHUNKS = 8
CENTRE, KAPPA, EAST, NORTH, OCEAN = range(5)
KAPPA_W, KAPPA_E, KAPPA_S, KAPPA_N, EAST_W, EAST_E, NORTH_S, NORTH_N = range(5, 13)


def rolled(value, by, axis):
    return pltpu.roll(value, by % value.shape[axis], axis)


def kernel(
    n_lat,
    n_coh,
    dens_in,
    cot_in,
    land,
    east,
    north,
    diff,
    age,
    mort,
    crowd_coef,
    mass,
    speed,
    out,
    out_press,
    out_grads,
    dens,
    cot,
    last,
    field,
    halo_field,
    params,
    state,
    surv1,
    wet1,
    surv2,
    wet2,
    lap1,
    east1,
    north1,
    kept,
    total,
    partial,
    arrived,
    grads,
    share,
    share_in,
    dens_edge,
    field_o,
    field_h,
    cot1_o,
    cot1_h,
    cot2_o,
    cot2_h,
    part_o,
    part_h,
    crowd_o,
    crowd_h,
    press_o,
    press_h,
    edge_o,
    edge_h,
    edge_sum,
    beyond_o,
    beyond_in,
    outside,
    wet_edge,
    wet1_edge,
    inflow,
    adj_h,
    kept_h,
    alive_h,
    added_h,
    local_sem,
    lat_send,
    lat_recv,
    coh_send,
    coh_recv,
):
    cohorts, layers, rows, lon = dens.shape
    chunk = cohorts // CHUNKS

    def fetch(source, target, which):
        return [
            pltpu.make_async_copy(
                source.at[pl.ds(at * chunk, chunk)],
                target.at[pl.ds(at * chunk, chunk)],
                local_sem.at[which, at],
            )
            for at in range(CHUNKS)
        ]

    get_dens = fetch(dens_in, dens, 0)
    get_cot = fetch(cot_in, cot, 1)
    for copy in get_dens + get_cot:
        copy.start()
    every = cohorts * n_coh
    lat = lax.axis_index("lat")
    coh = lax.axis_index("coh")
    has_low = lat > 0
    has_high = lat < n_lat - 1
    low = jnp.maximum(lat - 1, 0)
    high = jnp.minimum(lat + 1, n_lat - 1)
    peers = [lax.rem(coh + by, n_coh) for by in range(1, n_coh)]

    barrier = pltpu.get_barrier_semaphore()
    for peer in peers:
        pl.semaphore_signal(barrier, inc=1, device_id={"coh": peer}, device_id_type=MESH)

    @pl.when(has_low)
    def _():
        pl.semaphore_signal(barrier, inc=1, device_id={"lat": low}, device_id_type=MESH)

    @pl.when(has_high)
    def _():
        pl.semaphore_signal(barrier, inc=1, device_id={"lat": high}, device_id_type=MESH)

    buffers = {
        FIELDS: (field_o, field_h),
        COT1: (cot1_o, cot1_h),
        COT2: (cot2_o, cot2_h),
        PART2: (part_o, part_h),
        CROWD2: (crowd_o, crowd_h),
        PRESS2: (press_o, press_h),
        EDGE: (edge_o, edge_h),
    }

    def message(kind, layer):
        outgoing, incoming = buffers[kind]

        def one(side, device):
            return pltpu.make_async_remote_copy(
                src_ref=outgoing.at[side, layer],
                dst_ref=incoming.at[1 - side, layer],
                send_sem=lat_send.at[kind, layer, side],
                recv_sem=lat_recv.at[kind, layer, 1 - side],
                device_id={"lat": device},
                device_id_type=MESH,
            )

        return one(0, low), one(1, high)

    def send(kind, layer):
        to_low, to_high = message(kind, layer)

        @pl.when(has_low)
        def _():
            to_low.start()

        @pl.when(has_high)
        def _():
            to_high.start()

    def receive(kind, layer):
        to_low, to_high = message(kind, layer)

        @pl.when(has_low)
        def _():
            to_high.wait_recv()

        @pl.when(has_high)
        def _():
            to_low.wait_recv()

    def sent(kind, layer):
        to_low, to_high = message(kind, layer)

        @pl.when(has_low)
        def _():
            to_low.wait_send()

        @pl.when(has_high)
        def _():
            to_high.wait_send()

    def to_peers(kind, layer, source, target):
        return [
            pltpu.make_async_remote_copy(
                src_ref=source(peer),
                dst_ref=target(by),
                send_sem=coh_send.at[kind, layer, by],
                recv_sem=coh_recv.at[kind, layer, by],
                device_id={"coh": peer},
                device_id_type=MESH,
            )
            for by, peer in enumerate(peers)
        ]

    def exchange(which, layer):
        return to_peers(
            which,
            layer,
            lambda peer: partial.at[which, layer],
            lambda by: arrived.at[which, by, layer],
        )

    def exchange_beyond(layer):
        return to_peers(
            2 * STEPS, layer, lambda peer: beyond_o.at[layer], lambda by: beyond_in.at[by, layer]
        )

    def exchange_share(layer):
        return to_peers(
            2 * STEPS + 1,
            layer,
            lambda peer: share.at[peer, layer],
            lambda by: share_in.at[by, layer],
        )

    def begin(copies):
        for copy in copies:
            copy.start()

    def summed(which, layer):
        for copy in exchange(which, layer):
            copy.wait_recv()
        value = partial[which, layer]
        for by in range(n_coh - 1):
            value = value + arrived[which, by, layer]
        total[which, layer] = value * (1.0 / every)

    def pack(source, layer, low_row, high_row, target):
        def body(step, carry):
            for member in range(GROUP):
                cohort = step * GROUP + member
                spot = pl.ds(cohort, 1)
                target[0, layer, spot, :] = source[cohort, layer, low_row : low_row + 1, :]
                target[1, layer, spot, :] = source[cohort, layer, high_row : high_row + 1, :]
            return carry

        lax.fori_loop(0, cohorts // GROUP, body, 0)

    for layer in range(layers):
        raw = (land[layer].astype(jnp.float32), east[layer], north[layer], diff[layer])
        for index, value in enumerate(raw):
            for depth in range(2):
                spot = slice(2 * index + depth, 2 * index + depth + 1)
                field_o[0, layer, spot, :] = value[depth : depth + 1]
                field_o[1, layer, spot, :] = value[rows - 1 - depth : rows - depth]

    for side, exists in ((0, has_low), (1, has_high)):

        @pl.when(jnp.logical_not(exists))
        def _(side=side):
            for _, target in buffers.values():
                target[side] = jnp.zeros(target.shape[1:], jnp.float32)

    pl.semaphore_wait(
        barrier, n_coh - 1 + has_low.astype(jnp.int32) + has_high.astype(jnp.int32)
    )
    for layer in range(layers):
        send(FIELDS, layer)
    for copy in get_dens:
        copy.wait()

    chunks = lon // LANES
    lane = lax.broadcasted_iota(jnp.int32, (8, LANES), 1)
    leftmost = lane == 0
    rightmost = lane == LANES - 1
    row = lax.broadcasted_iota(jnp.int32, (rows, LANES), 0)
    is_first = row == 0
    is_last = row == rows - 1
    zero = jnp.zeros((rows, LANES), jnp.float32)

    def lanes_of(at):
        return pl.ds(pl.multiple_of(at * LANES, LANES), LANES)

    def over_chunks(body):
        def one(at, carry):
            west, east = lax.rem(at + (chunks - 1), chunks), lax.rem(at + 1, chunks)
            body(lanes_of(at), lanes_of(west), lanes_of(east))
            return carry

        lax.fori_loop(0, chunks, one, 0)

    def over_cohorts(body, carry):
        def one(step, carry):
            first = pl.multiple_of(step * GROUP, 8)
            for member in range(GROUP):
                eight = pl.ds(pl.multiple_of(first + member // 8 * 8, 8), 8)
                carry = body(first + member, (eight, member % 8), carry)
            return carry

        return lax.fori_loop(0, cohorts // GROUP, one, carry)

    def at_west(here, west):
        return pltpu.roll(jnp.where(rightmost, west, here), 1, 1)

    def at_east(here, east):
        return pltpu.roll(jnp.where(leftmost, east, here), LANES - 1, 1)

    for layer in range(layers):

        def weigh_chunk(here, west, east, layer=layer):
            def weigh(cohort, spot, sums):
                return sums + mass[age[cohort]] * dens[cohort, layer, :, here]

            partial[0, layer, :, here] = over_cohorts(weigh, zero)

        over_chunks(weigh_chunk)
        begin(exchange(0, layer))

    for layer in range(layers):
        ocean = land[layer].astype(jnp.float32)
        kappa = diff[layer]
        field[CENTRE, layer] = ocean * (1.0 - 4.0 * kappa)
        field[KAPPA, layer] = ocean * kappa
        field[EAST, layer] = ocean * (0.5 * east[layer])
        field[NORTH, layer] = ocean * (0.5 * north[layer])
        field[OCEAN, layer] = ocean
    for cohort in range(cohorts):
        one = age[cohort]
        for index, table in enumerate((mort, crowd_coef, mass, speed)):
            params[index, cohort : cohort + 1, :] = jnp.full((1, 128), table[one], jnp.float32)
    for copy in get_cot:
        copy.wait()
    for layer in range(layers):
        pack(cot, layer, 0, rows - 1, cot1_o)
        send(COT1, layer)
    for layer in range(layers):
        pack(cot, layer, 1, rows - 2, cot2_o)
        send(COT2, layer)
    for layer in range(layers):
        pack(dens, layer, 0, rows - 1, dens_edge)

    def wide(index, first):
        return params[index, first : first + 8, :]

    def over_edges(body):
        def one(here, west, east):
            for side in range(2):
                body(side, here, west, east)

        over_chunks(one)

    def spread(value):
        return jnp.broadcast_to(value, (8, LANES))

    def halo_row(side, index, depth, layer, here):
        spot = 2 * index + depth if index < 5 else index + 5
        return spread(halo_field[side, layer, spot : spot + 1, here])

    for layer in range(layers):
        receive(FIELDS, layer)
        for side in range(2):
            raw = [field_h[side, layer, 2 * index : 2 * index + 2] for index in range(4)]
            ocean, kappa = raw[0], raw[3]
            values = (
                ocean * (1.0 - 4.0 * kappa),
                ocean * kappa,
                ocean * (0.5 * raw[1]),
                ocean * (0.5 * raw[2]),
                ocean,
            )
            for index, value in enumerate(values):
                halo_field[side, layer, 2 * index : 2 * index + 2] = value
            near = [value[:1] for value in values]
            for index, by in ((KAPPA_W, 1), (KAPPA_E, -1), (EAST_W, 1), (EAST_E, -1)):
                base = near[KAPPA] if index in (KAPPA_W, KAPPA_E) else near[EAST]
                halo_field[side, layer, index + 5 : index + 6] = rolled(base, by, 1)
        kappa, drift, climb = field[KAPPA, layer], field[EAST, layer], field[NORTH, layer]
        field[KAPPA_W, layer] = rolled(kappa, 1, 1)
        field[KAPPA_E, layer] = rolled(kappa, -1, 1)
        field[EAST_W, layer] = rolled(drift, 1, 1)
        field[EAST_E, layer] = rolled(drift, -1, 1)
        field[KAPPA_S, layer] = rolled(kappa, 1, 0)
        field[KAPPA_N, layer] = rolled(kappa, -1, 0)
        field[NORTH_S, layer] = rolled(climb, 1, 0)
        field[NORTH_N, layer] = rolled(climb, -1, 0)
        for index, origin in ((KAPPA_S, KAPPA), (NORTH_S, NORTH)):
            field[index, layer, :1] = halo_field[0, layer, 2 * origin : 2 * origin + 1]
        for index, origin in ((KAPPA_N, KAPPA), (NORTH_N, NORTH)):
            field[index, layer, rows - 1 :] = halo_field[1, layer, 2 * origin : 2 * origin + 1]

    def inner(side):
        return slice(0, 1) if side == 0 else slice(rows - 1, rows)

    def column(value):
        return jnp.sum(value, axis=0, keepdims=True)

    def from_before(value, edge):
        return jnp.where(is_first, edge, rolled(value, 1, 0))

    def from_after(value, edge):
        return jnp.where(is_last, edge, rolled(value, -1, 0))

    def edge_row(ref, side, layer, spot, here):
        eight, member = spot
        return ref[side, layer, eight, here][member : member + 1]

    def whole_rows(first_edge, last_edge):
        full = lax.broadcasted_iota(jnp.int32, (rows, lon), 0)
        return jnp.where(full == 0, first_edge, 0.0) + jnp.where(full == rows - 1, last_edge, 0.0)

    def survive(layer, which, start, alive_ref, wet_ref, edges):
        def one(here, west, east):
            ocean = field[OCEAN, layer, :, here]
            crowd = total[which, layer, :, here]
            held = []

            def each(cohort, spot, carry):
                age_of = age[cohort]
                alive = ocean * jnp.exp(-(mort[age_of] + crowd_coef[age_of] * crowd))
                wet = start[cohort, layer, :, here] * alive
                alive_ref[cohort, layer, :, here] = alive
                wet_ref[cohort, layer, :, here] = wet
                if edges:
                    eight, member = spot
                    if member == 0:
                        held.clear()
                    held.append(wet)
                    if member == 7:
                        for side in range(2):
                            edge = [value[inner(side)] for value in held]
                            wet_edge[side, layer, eight, here] = jnp.concatenate(edge, axis=0)
                return carry

            over_cohorts(each, 0)

        over_chunks(one)

    def first_step(layer):
        summed(0, layer)

        def outflow(side, here, west, east):
            crowd = spread(total[0, layer, inner(side), here])
            ocean = spread(field[OCEAN, layer, inner(side), here])
            climb = halo_row(side, NORTH, 0, layer, here)
            kappa = halo_row(side, KAPPA, 0, layer, here)
            sums = jnp.zeros((8, LANES), jnp.float32)
            for first in range(0, cohorts, 8):
                spot = pl.ds(first, 8)
                alive = ocean * jnp.exp(-(wide(0, first) + wide(1, first) * crowd))
                wet = dens_edge[side, layer, spot, here] * alive
                shift = wide(3, first) * climb
                coef = kappa - shift if side == 0 else kappa + shift
                value = coef * wet
                wet1_edge[side, layer, spot, here] = wet
                inflow[side, layer, spot, here] = value
                sums = sums + wide(2, first) * value
            part_o[side, layer, :, here] = column(sums)

        over_edges(outflow)
        send(PART2, layer)
        survive(layer, 0, dens, surv1, wet1, False)

        def forward_chunk(here, west, east):
            centre, kappa, drift, climb = (field[index, layer, :, here] for index in range(4))

            def forward(cohort, spot, sums):
                age_of = age[cohort]
                wet = wet1[cohort, layer, :, here]
                west_val = at_west(wet, wet1[cohort, layer, :, west])
                east_val = at_east(wet, wet1[cohort, layer, :, east])
                before = from_before(wet, 0.0)
                after = from_after(wet, 0.0)
                around = (before + after) + (west_val + east_val)
                east_diff = east_val - west_val
                north_diff = after - before
                value = (centre * wet + kappa * around) - speed[age_of] * (
                    drift * east_diff + climb * north_diff
                )
                lap1[cohort, layer, :, here] = around - 4.0 * wet
                east1[cohort, layer, :, here] = east_diff
                north1[cohort, layer, :, here] = north_diff
                state[cohort, layer, :, here] = value
                return sums + mass[age_of] * value

            partial[1, layer, :, here] = over_cohorts(forward, zero)

        over_chunks(forward_chunk)
        receive(PART2, layer)
        partial[1, layer] += whole_rows(part_h[0, layer], part_h[1, layer])
        begin(exchange(1, layer))

    def pulled(coefs, swim, here, west, east, south, north):
        return (
            coefs[0] * here
            + (coefs[1] * west + coefs[2] * east)
            + (coefs[3] * south + coefs[4] * north)
            - swim * ((coefs[5] * west - coefs[6] * east) + (coefs[7] * south - coefs[8] * north))
        )

    def gathered(layer, here):
        indices = (CENTRE, KAPPA_W, KAPPA_E, KAPPA_S, KAPPA_N, EAST_W, EAST_E, NORTH_S, NORTH_N)
        return [field[index, layer, :, here] for index in indices]

    def second_back(layer):
        summed(1, layer)
        for side in range(2):
            crowd_o[side, layer] = total[1, layer, inner(side), :]
        send(CROWD2, layer)
        survive(layer, 1, state, surv2, wet2, True)
        receive(COT1, layer)

        def back2_chunk(here, west, east):
            coefs = gathered(layer, here)

            def back2(cohort, spot, sums):
                age_of = age[cohort]
                swim = speed[age_of]
                wet = wet2[cohort, layer, :, here]
                west_val = at_west(wet, wet2[cohort, layer, :, west])
                east_val = at_east(wet, wet2[cohort, layer, :, east])
                before = from_before(wet, 0.0)
                after = from_after(wet, 0.0)
                adjoint = cot[cohort, layer, :, here]
                swum = swim * adjoint
                pull = pulled(
                    coefs,
                    swim,
                    adjoint,
                    at_west(adjoint, cot[cohort, layer, :, west]),
                    at_east(adjoint, cot[cohort, layer, :, east]),
                    from_before(adjoint, edge_row(cot1_h, 0, layer, spot, here)),
                    from_after(adjoint, edge_row(cot1_h, 1, layer, spot, here)),
                )
                kept[cohort, layer, :, here] = pull * surv2[cohort, layer, :, here]
                return (
                    sums[0] + swum * (east_val - west_val),
                    sums[1] + swum * (after - before),
                    sums[2] + adjoint * ((before + after) + (west_val + east_val) - 4.0 * wet),
                    sums[3] - crowd_coef[age_of] * (pull * wet),
                )

            sums = over_cohorts(back2, (zero,) * 4)
            for index in range(3):
                grads[index, layer, :, here] = sums[index]
            partial[2, layer, :, here] = sums[3]

        over_chunks(back2_chunk)
        begin(exchange(2, layer))

    def second_beyond(layer):
        receive(CROWD2, layer)

        def survive_halo(side, here, west, east):
            crowd = spread(crowd_h[side, layer, :, here])
            ocean = halo_row(side, OCEAN, 0, layer, here)
            for first in range(0, cohorts, 8):
                spot = pl.ds(first, 8)
                alive = ocean * jnp.exp(-(wide(0, first) + wide(1, first) * crowd))
                alive_h[side, layer, spot, here] = alive
                added_h[side, layer, spot, here] = inflow[side, layer, spot, here] * alive

        over_edges(survive_halo)
        receive(COT2, layer)

        def back2_halo(side, here, west, east):
            sign = 1.0 if side == 0 else -1.0
            centre, kappa_w, kappa_e, drift_w, drift_e = (
                halo_row(side, index, 0, layer, here)
                for index in (CENTRE, KAPPA_W, KAPPA_E, EAST_W, EAST_E)
            )
            outer_kappa = halo_row(side, KAPPA, 1, layer, here)
            outer_climb = sign * halo_row(side, NORTH, 1, layer, here)
            inner_kappa = spread(field[KAPPA, layer, inner(side), here])
            inner_climb = sign * spread(field[NORTH, layer, inner(side), here])
            sums = [jnp.zeros((8, LANES), jnp.float32)] * 8
            for first in range(0, cohorts, 8):
                spot = pl.ds(first, 8)
                swim = wide(3, first)
                adjoint = cot1_h[side, layer, spot, here]
                behind = cot2_h[side, layer, spot, here]
                ours = cot1_o[side, layer, spot, here]
                adj_w = at_west(adjoint, cot1_h[side, layer, spot, west])
                adj_e = at_east(adjoint, cot1_h[side, layer, spot, east])
                pull = (
                    centre * adjoint
                    + (kappa_w * adj_w + kappa_e * adj_e)
                    + (outer_kappa * behind + inner_kappa * ours)
                    - swim
                    * ((drift_w * adj_w - drift_e * adj_e) + (outer_climb * behind - inner_climb * ours))
                )
                kept_h[side, layer, spot, here] = pull * alive_h[side, layer, spot, here]
                added = added_h[side, layer, spot, here]
                west_val = at_west(added, added_h[side, layer, spot, west])
                east_val = at_east(added, added_h[side, layer, spot, east])
                wet = wet_edge[side, layer, spot, here]
                swum = swim * adjoint
                far, own = behind * added, ours * added
                for index, value in (
                    (KAPPA_NEAR, adjoint * (wet + (west_val + east_val) - 4.0 * added)),
                    (NORTH_NEAR, swum * wet),
                    (EAST_NEAR, swum * (east_val - west_val)),
                    (KAPPA_FAR, far),
                    (NORTH_FAR, swim * far),
                    (KAPPA_OWN, own),
                    (NORTH_OWN, swim * own),
                    (7, wide(1, first) * (pull * added)),
                ):
                    sums[index] = sums[index] + value
            for index in range(7):
                edge_sum[side, layer, index : index + 1, here] = column(sums[index])
            beyond_o[layer, side : side + 1, here] = -column(sums[7])

        over_edges(back2_halo)
        begin(exchange_beyond(layer))

    def second_pressure(layer):
        summed(2, layer)
        for copy in exchange_beyond(layer):
            copy.wait_recv()
        value = beyond_o[layer]
        for by in range(n_coh - 1):
            value = value + beyond_in[by, layer]
        value = value * (1.0 / every)
        outside[layer] = value
        for side in range(2):
            press_o[side, layer, :1] = total[2, layer, inner(side), :]
            press_o[side, layer, 1:] = value[side : side + 1]
        send(PRESS2, layer)

    def first_back(layer):
        receive(PRESS2, layer)
        total[2, layer] += whole_rows(press_h[0, layer, 1:], press_h[1, layer, 1:])

        def inflow_first(side, here, west, east):
            pressure = spread(press_h[side, layer, :1, here] + outside[layer, side : side + 1, here])
            sums = [jnp.zeros((8, LANES), jnp.float32)] * 2
            for first in range(0, cohorts, 8):
                spot = pl.ds(first, 8)
                adjoint = kept_h[side, layer, spot, here] + wide(2, first) * pressure
                adj_h[side, layer, spot, here] = adjoint
                product = adjoint * wet1_edge[side, layer, spot, here]
                sums = [sums[0] + product, sums[1] + wide(3, first) * product]
            for index in range(SENT):
                value = edge_sum[side, layer, index : index + 1, here]
                if index in (KAPPA_NEAR, NORTH_NEAR):
                    value = value + column(sums[index])
                edge_o[side, layer, index : index + 1, here] = value

        over_edges(inflow_first)
        send(EDGE, layer)

        def back1_chunk(here, west, east):
            coefs = gathered(layer, here)
            press = total[2, layer, :, here]
            press_w = jnp.where(rightmost, total[2, layer, :, west], press)
            press_e = jnp.where(leftmost, total[2, layer, :, east], press)

            def back1(cohort, spot, sums):
                age_of = age[cohort]
                swim, weight = speed[age_of], mass[age_of]
                held = kept[cohort, layer, :, here]
                adjoint = held + weight * press
                adj_w = jnp.where(rightmost, kept[cohort, layer, :, west], held) + weight * press_w
                adj_e = jnp.where(leftmost, kept[cohort, layer, :, east], held) + weight * press_e
                swum = swim * adjoint
                pull = pulled(
                    coefs,
                    swim,
                    adjoint,
                    pltpu.roll(adj_w, 1, 1),
                    pltpu.roll(adj_e, LANES - 1, 1),
                    from_before(adjoint, edge_row(adj_h, 0, layer, spot, here)),
                    from_after(adjoint, edge_row(adj_h, 1, layer, spot, here)),
                )
                last[cohort, layer, :, here] = pull * surv1[cohort, layer, :, here]
                return (
                    sums[0] + swum * east1[cohort, layer, :, here],
                    sums[1] + swum * north1[cohort, layer, :, here],
                    sums[2] + adjoint * lap1[cohort, layer, :, here],
                    sums[3] - crowd_coef[age_of] * (pull * wet1[cohort, layer, :, here]),
                )

            sums = over_cohorts(back1, (zero,) * 4)
            for index in range(3):
                grads[index, layer, :, here] += sums[index]
            partial[3, layer, :, here] = sums[3]

        over_chunks(back1_chunk)
        begin(exchange(3, layer))

    def put(layer):
        return [
            pltpu.make_async_copy(
                last.at[pl.ds(at * chunk, chunk), layer],
                out.at[pl.ds(at * chunk, chunk), layer],
                local_sem.at[2 + layer, at],
            )
            for at in range(CHUNKS)
        ]

    part = lon // n_coh

    def gradients(layer):
        receive(EDGE, layer)
        ocean = field[OCEAN, layer]
        full = lax.broadcasted_iota(jnp.int32, (rows, lon), 0)
        near = (full == 0, full == rows - 1)
        behind = (full == 1, full == rows - 2)
        drift, climb, kappa = (grads[index, layer] for index in range(3))
        for side in range(2):

            def got(index):
                return edge_h[side, layer, index : index + 1, :]

            def own(index):
                return edge_sum[side, layer, index : index + 1, :]

            sign = -1.0 if side == 0 else 1.0
            kappa_near = got(KAPPA_NEAR) + own(KAPPA_OWN)
            north_near = sign * (got(NORTH_NEAR) + own(NORTH_OWN))
            drift = drift + jnp.where(near[side], got(EAST_NEAR), 0.0)
            climb = climb + jnp.where(near[side], north_near, 0.0)
            climb = climb + jnp.where(behind[side], sign * got(NORTH_FAR), 0.0)
            kappa = kappa + jnp.where(near[side], kappa_near, 0.0)
            kappa = kappa + jnp.where(behind[side], got(KAPPA_FAR), 0.0)
        values = (-0.5 * ocean * drift, -0.5 * ocean * climb, ocean * kappa)
        for index, value in enumerate(values):
            for to in range(n_coh):
                share[to, layer, index] = value[:, to * part : (to + 1) * part]
        begin(exchange_share(layer))

    for layer in range(layers):
        first_step(layer)
    for layer in range(layers):
        second_back(layer)
        if layer > 0:
            second_pressure(layer - 1)
        second_beyond(layer)
    for layer in range(layers):
        if layer == layers - 1:
            second_pressure(layer)
        if layer > 0:
            gradients(layer - 1)
        first_back(layer)
        begin(put(layer))
    gradients(layers - 1)
    for layer in range(layers):
        summed(3, layer)
        out_press[layer] = total[3, layer]
        for copy in exchange_share(layer):
            copy.wait_recv()
        for index in range(3):
            value = share[coh, layer, index]
            for by in range(n_coh - 1):
                value = value + share_in[by, layer, index]
            out_grads[index, layer] = value

    for layer in range(layers):
        for copy in put(layer):
            copy.wait()
        for kind in buffers:
            sent(kind, layer)
        for which in range(2 * STEPS):
            for copy in exchange(which, layer):
                copy.wait_send()
        for copy in exchange_beyond(layer) + exchange_share(layer):
            copy.wait_send()


def finish(age, mass, last, press, grads, out, out_east, out_north, out_kappa, held, sem):
    cohorts, layers = held.shape[:2]
    chunk = cohorts // CHUNKS
    spots = [pl.ds(at * chunk, chunk) for at in range(CHUNKS)]
    get = [
        pltpu.make_async_copy(last.at[spot], held.at[spot], sem.at[0, at])
        for at, spot in enumerate(spots)
    ]
    put = [
        pltpu.make_async_copy(held.at[spot], out.at[spot], sem.at[1, at])
        for at, spot in enumerate(spots)
    ]
    for copy in get:
        copy.start()
    for index, target in enumerate((out_east, out_north, out_kappa)):
        target[...] = grads[index]
    for at in range(CHUNKS):
        get[at].wait()
        for cohort in range(at * chunk, (at + 1) * chunk):
            weight = mass[age[cohort]]
            for layer in range(layers):
                held[cohort, layer] += weight * press[layer]
        put[at].start()
    for copy in put:
        copy.wait()


def local(*args):
    density = args[0]
    cohorts, layers, rows, lon = density.shape
    n_lat, n_coh = lax.axis_size("lat"), lax.axis_size("coh")
    f32 = jnp.float32
    vmem = pl.BlockSpec(memory_space=pltpu.VMEM)
    smem = pl.BlockSpec(memory_space=pltpu.SMEM)
    share = jax.ShapeDtypeStruct((layers, rows, lon // n_coh), f32)
    whole = pltpu.VMEM(density.shape, f32)
    packed = pltpu.VMEM((2, layers, cohorts, lon), f32)
    def vec(*shape):
        return pltpu.VMEM(shape, f32)

    part = lon // n_coh
    hbm = pl.BlockSpec(memory_space=pl.ANY)
    scratch = (
        [whole] * 3
        + [
            vec(13, layers, rows, lon),
            vec(2, layers, 18, lon),
            vec(4, cohorts, 128),
        ]
        + [whole] * 9
        + [
            vec(4, layers, rows, lon),
            vec(4, layers, rows, lon),
            vec(4, n_coh - 1, layers, rows, lon),
            vec(3, layers, rows, lon),
            vec(n_coh, layers, 3, rows, part),
            vec(n_coh - 1, layers, 3, rows, part),
            packed,
            vec(2, layers, 8, lon),
            vec(2, layers, 8, lon),
            packed,
            packed,
            packed,
            packed,
            vec(2, layers, 1, lon),
            vec(2, layers, 1, lon),
            vec(2, layers, 1, lon),
            vec(2, layers, 1, lon),
            vec(2, layers, 2, lon),
            vec(2, layers, 2, lon),
            vec(2, layers, SENT, lon),
            vec(2, layers, SENT, lon),
            vec(2, layers, 7, lon),
            vec(layers, 2, lon),
            vec(n_coh - 1, layers, 2, lon),
            vec(layers, 2, lon),
        ]
        + [packed] * 7
        + [
            pltpu.SemaphoreType.DMA((2 + layers, CHUNKS)),
            pltpu.SemaphoreType.DMA((7, layers, 2)),
            pltpu.SemaphoreType.DMA((7, layers, 2)),
            pltpu.SemaphoreType.DMA((6, layers, n_coh - 1)),
            pltpu.SemaphoreType.DMA((6, layers, n_coh - 1)),
        ]
    )
    size = density.size
    last, press, grads = pl.pallas_call(
        functools.partial(kernel, n_lat, n_coh),
        out_shape=(
            jax.ShapeDtypeStruct(density.shape, f32),
            jax.ShapeDtypeStruct((layers, rows, lon), f32),
            jax.ShapeDtypeStruct((3, layers, rows, part), f32),
        ),
        in_specs=[hbm] * 2 + [vmem] * 4 + [smem] * 5,
        out_specs=(hbm, vmem, vmem),
        scratch_shapes=scratch,
        compiler_params=pltpu.CompilerParams(
            collective_id=0, has_side_effects=True, vmem_limit_bytes=56 * 1024 * 1024
        ),
        cost_estimate=pl.CostEstimate(
            flops=150 * size, bytes_accessed=12 * size, transcendentals=2 * size
        ),
    )(*args)
    return pl.pallas_call(
        finish,
        out_shape=(jax.ShapeDtypeStruct(density.shape, f32), share, share, share),
        in_specs=[smem, smem, hbm, vmem, vmem],
        out_specs=(hbm, vmem, vmem, vmem),
        scratch_shapes=[whole, pltpu.SemaphoreType.DMA((2, CHUNKS))],
        compiler_params=pltpu.CompilerParams(vmem_limit_bytes=56 * 1024 * 1024),
        cost_estimate=pl.CostEstimate(flops=2 * size, bytes_accessed=8 * size, transcendentals=0),
    )(args[6], args[9], last, press, grads)


def solution(mesh):
    fields = P(None, "lat", None)
    in_specs = (P("coh", None, "lat", None),) * 2 + (fields,) * 4 + (P("coh"),) + (P(),) * 4
    out_specs = (P("coh", None, "lat", None),) + (P(None, "lat", "coh"),) * 3
    return jax.shard_map(local, mesh=mesh, in_specs=in_specs, out_specs=out_specs, check_vma=False)
```

```python
import functools

import jax
import jax.numpy as jnp
from jax import lax
from jax.experimental import pallas as pl
from jax.experimental.pallas import tpu as pltpu
from jax.sharding import PartitionSpec as P

STEPS = 2
MESH = pl.DeviceIdType.MESH
FIELDS, COT1, COT2, PART2, CROWD2, PRESS2, EDGE = range(7)
KAPPA_NEAR, NORTH_NEAR, EAST_NEAR, KAPPA_FAR, NORTH_FAR, KAPPA_OWN, NORTH_OWN = range(7)
SENT = 5
GROUP = 4
CHUNKS = 8
CENTRE, KAPPA, EAST, NORTH, OCEAN = range(5)


def rolled(value, by, axis):
    return pltpu.roll(value, by % value.shape[axis], axis)


def kernel(
    n_lat,
    n_coh,
    dens_in,
    cot_in,
    land,
    east,
    north,
    diff,
    age,
    mort,
    crowd_coef,
    mass,
    speed,
    out,
    out_press,
    out_grads,
    dens,
    cot,
    last,
    field,
    halo_field,
    params,
    state,
    surv1,
    wet1,
    lap1,
    east1,
    north1,
    kept,
    total,
    partial,
    arrived,
    grads,
    share,
    share_in,
    dens_edge,
    field_o,
    field_h,
    cot1_o,
    cot1_h,
    cot2_o,
    cot2_h,
    part_o,
    part_h,
    crowd_o,
    crowd_h,
    press_o,
    press_h,
    edge_o,
    edge_h,
    edge_sum,
    beyond,
    beyond_o,
    beyond_in,
    outside,
    wet_edge,
    wet1_edge,
    coefs,
    inflow,
    into,
    kept_h,
    local_sem,
    lat_send,
    lat_recv,
    coh_send,
    coh_recv,
):
    cohorts, layers, rows, lon = dens.shape
    chunk = cohorts // CHUNKS

    def fetch(source, target, which):
        return [
            pltpu.make_async_copy(
                source.at[pl.ds(at * chunk, chunk)],
                target.at[pl.ds(at * chunk, chunk)],
                local_sem.at[which, at],
            )
            for at in range(CHUNKS)
        ]

    get_dens = fetch(dens_in, dens, 0)
    get_cot = fetch(cot_in, cot, 1)
    for copy in get_cot + get_dens:
        copy.start()
    every = cohorts * n_coh
    lat = lax.axis_index("lat")
    coh = lax.axis_index("coh")
    has_low = lat > 0
    has_high = lat < n_lat - 1
    low = jnp.maximum(lat - 1, 0)
    high = jnp.minimum(lat + 1, n_lat - 1)
    peers = [lax.rem(coh + by, n_coh) for by in range(1, n_coh)]

    barrier = pltpu.get_barrier_semaphore()
    for peer in peers:
        pl.semaphore_signal(barrier, inc=1, device_id={"coh": peer}, device_id_type=MESH)

    @pl.when(has_low)
    def _():
        pl.semaphore_signal(barrier, inc=1, device_id={"lat": low}, device_id_type=MESH)

    @pl.when(has_high)
    def _():
        pl.semaphore_signal(barrier, inc=1, device_id={"lat": high}, device_id_type=MESH)

    buffers = {
        FIELDS: (field_o, field_h),
        COT1: (cot1_o, cot1_h),
        COT2: (cot2_o, cot2_h),
        PART2: (part_o, part_h),
        CROWD2: (crowd_o, crowd_h),
        PRESS2: (press_o, press_h),
        EDGE: (edge_o, edge_h),
    }

    def message(kind, layer):
        outgoing, incoming = buffers[kind]

        def one(side, device):
            return pltpu.make_async_remote_copy(
                src_ref=outgoing.at[side, layer],
                dst_ref=incoming.at[1 - side, layer],
                send_sem=lat_send.at[kind, layer, side],
                recv_sem=lat_recv.at[kind, layer, 1 - side],
                device_id={"lat": device},
                device_id_type=MESH,
            )

        return one(0, low), one(1, high)

    def send(kind, layer):
        to_low, to_high = message(kind, layer)

        @pl.when(has_low)
        def _():
            to_low.start()

        @pl.when(has_high)
        def _():
            to_high.start()

    def receive(kind, layer):
        to_low, to_high = message(kind, layer)

        @pl.when(has_low)
        def _():
            to_high.wait_recv()

        @pl.when(has_high)
        def _():
            to_low.wait_recv()

    def sent(kind, layer):
        to_low, to_high = message(kind, layer)

        @pl.when(has_low)
        def _():
            to_low.wait_send()

        @pl.when(has_high)
        def _():
            to_high.wait_send()

    def to_peers(kind, layer, source, target):
        return [
            pltpu.make_async_remote_copy(
                src_ref=source(peer),
                dst_ref=target(by),
                send_sem=coh_send.at[kind, layer, by],
                recv_sem=coh_recv.at[kind, layer, by],
                device_id={"coh": peer},
                device_id_type=MESH,
            )
            for by, peer in enumerate(peers)
        ]

    def exchange(which, layer):
        return to_peers(
            which,
            layer,
            lambda peer: partial.at[which, layer],
            lambda by: arrived.at[which, by, layer],
        )

    def exchange_beyond(layer):
        return to_peers(
            2 * STEPS, layer, lambda peer: beyond_o.at[layer], lambda by: beyond_in.at[by, layer]
        )

    def exchange_share(layer):
        return to_peers(
            2 * STEPS + 1,
            layer,
            lambda peer: share.at[peer, layer],
            lambda by: share_in.at[by, layer],
        )

    def begin(copies):
        for copy in copies:
            copy.start()

    def summed(which, layer):
        for copy in exchange(which, layer):
            copy.wait_recv()
        value = partial[which, layer]
        for by in range(n_coh - 1):
            value = value + arrived[which, by, layer]
        total[which, layer] = value * (1.0 / every)

    def pack(source, layer, low_row, high_row, target):
        def body(step, carry):
            for member in range(GROUP):
                cohort = step * GROUP + member
                spot = pl.ds(cohort, 1)
                target[0, layer, spot, :] = source[cohort, layer, low_row : low_row + 1, :]
                target[1, layer, spot, :] = source[cohort, layer, high_row : high_row + 1, :]
            return carry

        lax.fori_loop(0, cohorts // GROUP, body, 0)

    for layer in range(layers):
        raw = (land[layer].astype(jnp.float32), east[layer], north[layer], diff[layer])
        for index, value in enumerate(raw):
            for depth in range(2):
                spot = slice(2 * index + depth, 2 * index + depth + 1)
                field_o[0, layer, spot, :] = value[depth : depth + 1]
                field_o[1, layer, spot, :] = value[rows - 1 - depth : rows - depth]

    for side, exists in ((0, has_low), (1, has_high)):

        @pl.when(jnp.logical_not(exists))
        def _(side=side):
            for _, target in buffers.values():
                target[side] = jnp.zeros(target.shape[1:], jnp.float32)

    pl.semaphore_wait(
        barrier, n_coh - 1 + has_low.astype(jnp.int32) + has_high.astype(jnp.int32)
    )
    for layer in range(layers):
        send(FIELDS, layer)
    for copy in get_cot:
        copy.wait()
    for layer in range(layers):
        pack(cot, layer, 0, rows - 1, cot1_o)
        send(COT1, layer)
    for layer in range(layers):
        pack(cot, layer, 1, rows - 2, cot2_o)
        send(COT2, layer)
    for copy in get_dens:
        copy.wait()

    zero = jnp.zeros((rows, lon), jnp.float32)

    def over_cohorts(body):
        def one(step, carry):
            return body([step * GROUP + member for member in range(GROUP)], carry)

        return lax.fori_loop(0, cohorts // GROUP, one, zero)

    def added_up(values):
        value = values[0]
        for other in values[1:]:
            value = value + other
        return value

    for layer in range(layers):

        def weigh(group, sums, layer=layer):
            return sums + added_up([mass[age[cohort]] * dens[cohort, layer] for cohort in group])

        partial[0, layer] = over_cohorts(weigh)
        begin(exchange(0, layer))

    for layer in range(layers):
        ocean = land[layer].astype(jnp.float32)
        kappa = diff[layer]
        field[CENTRE, layer] = ocean * (1.0 - 4.0 * kappa)
        field[KAPPA, layer] = ocean * kappa
        field[EAST, layer] = ocean * (0.5 * east[layer])
        field[NORTH, layer] = ocean * (0.5 * north[layer])
        field[OCEAN, layer] = ocean
    for cohort in range(cohorts):
        one = age[cohort]
        for index, table in enumerate((mort, crowd_coef, mass, speed)):
            params[index, cohort : cohort + 1, :] = jnp.full((1, 128), table[one], jnp.float32)
    for layer in range(layers):
        pack(dens, layer, 0, rows - 1, dens_edge)
    grads[...] = jnp.zeros(grads.shape, jnp.float32)
    edge_sum[...] = jnp.zeros(edge_sum.shape, jnp.float32)
    beyond[...] = jnp.zeros(beyond.shape, jnp.float32)

    def wide(index, first):
        value = params[index, pl.ds(first, 8), :]
        return jnp.concatenate([value] * (lon // 128), axis=1)

    def spread(row):
        return jnp.broadcast_to(row, (8, lon))

    def over_groups(body):
        def one(group, carry):
            first = pl.multiple_of(group * 8, 8)
            body(first, pl.ds(first, 8))
            return carry

        lax.fori_loop(0, cohorts // 8, one, 0)

    def halo_row(side, index, depth, layer):
        return spread(halo_field[side, layer, 2 * index + depth : 2 * index + depth + 1, :])

    for layer in range(layers):
        receive(FIELDS, layer)
        for side in range(2):
            raw = [field_h[side, layer, 2 * index : 2 * index + 2] for index in range(4)]
            ocean, kappa = raw[0], raw[3]
            values = (
                ocean * (1.0 - 4.0 * kappa),
                ocean * kappa,
                ocean * (0.5 * raw[1]),
                ocean * (0.5 * raw[2]),
                ocean,
            )
            for index, value in enumerate(values):
                halo_field[side, layer, 2 * index : 2 * index + 2] = value

    def survival_h(side, first, layer):
        crowd = spread(crowd_h[side, layer])
        return halo_row(side, OCEAN, 0, layer) * jnp.exp(-(wide(0, first) + wide(1, first) * crowd))

    def inner(side):
        return slice(0, 1) if side == 0 else slice(rows - 1, rows)

    def column(value):
        return jnp.sum(value, axis=0, keepdims=True)

    row = lax.broadcasted_iota(jnp.int32, (rows, lon), 0)
    is_first = row == 0
    is_last = row == rows - 1

    def from_before(value, edge):
        return jnp.where(is_first, edge, rolled(value, 1, 0))

    def from_after(value, edge):
        return jnp.where(is_last, edge, rolled(value, -1, 0))

    def scalars(cohort):
        one = age[cohort]
        return mort[one], crowd_coef[one], mass[one], speed[one]

    def survival(layer, which, mortal, crowding):
        return field[OCEAN, layer] * jnp.exp(-(mortal + crowding * total[which, layer]))

    def first_step(layer):
        summed(0, layer)

        def outflow(first, spot):
            swim = wide(3, first)
            for side in range(2):
                crowd = spread(total[0, layer, inner(side), :])
                ocean = spread(field[OCEAN, layer, inner(side), :])
                alive = ocean * jnp.exp(-(wide(0, first) + wide(1, first) * crowd))
                wet = dens_edge[side, layer, spot, :] * alive
                shift = swim * halo_row(side, NORTH, 0, layer)
                kappa = halo_row(side, KAPPA, 0, layer)
                coef = kappa - shift if side == 0 else kappa + shift
                value = coef * wet
                wet1_edge[side, layer, spot, :] = wet
                coefs[side, layer, spot, :] = coef
                inflow[side, layer, spot, :] = value
                beyond[0, side, layer] += wide(2, first) * value

        over_groups(outflow)
        for side in range(2):
            part_o[side, layer] = column(beyond[0, side, layer])
        send(PART2, layer)

        def forward(group, sums):
            added = []
            for cohort in group:
                mortal, crowding, weight, swim = scalars(cohort)
                alive = survival(layer, 0, mortal, crowding)
                wet = dens[cohort, layer] * alive
                before = from_before(wet, 0.0)
                after = from_after(wet, 0.0)
                west_val = rolled(wet, 1, 1)
                east_val = rolled(wet, -1, 1)
                around = (before + after) + (west_val + east_val)
                east_diff = east_val - west_val
                north_diff = after - before
                value = (
                    field[CENTRE, layer] * wet
                    + field[KAPPA, layer] * around
                    - swim * (field[EAST, layer] * east_diff + field[NORTH, layer] * north_diff)
                )
                surv1[cohort, layer] = alive
                wet1[cohort, layer] = wet
                lap1[cohort, layer] = around - 4.0 * wet
                east1[cohort, layer] = east_diff
                north1[cohort, layer] = north_diff
                state[cohort, layer] = value
                added.append(weight * value)
            return sums + added_up(added)

        sums = over_cohorts(forward)
        receive(PART2, layer)
        partial[1, layer] = sums + (
            jnp.where(is_first, part_h[0, layer], 0.0) + jnp.where(is_last, part_h[1, layer], 0.0)
        )
        begin(exchange(1, layer))

    def pulled(adjoint, swum, layer, spot):
        spread_out = field[KAPPA, layer] * adjoint
        drift = field[EAST, layer] * swum
        climb = field[NORTH, layer] * swum
        return (
            field[CENTRE, layer] * adjoint
            + rolled(spread_out - drift, 1, 1)
            + rolled(spread_out + drift, -1, 1)
            + from_before(spread_out - climb, into[0, layer, spot, :])
            + from_after(spread_out + climb, into[1, layer, spot, :])
        )

    def second_back(layer):
        receive(COT1, layer)

        def inflow_cot(first, spot):
            for side in range(2):
                into[side, layer, spot, :] = coefs[side, layer, spot, :] * cot1_h[side, layer, spot, :]

        over_groups(inflow_cot)
        summed(1, layer)
        for side in range(2):
            crowd_o[side, layer] = total[1, layer, inner(side), :]
        send(CROWD2, layer)

        def back2(group, sums):
            added = []
            products = []
            for cohort in group:
                mortal, crowding, weight, swim = scalars(cohort)
                spot = pl.ds(cohort, 1)
                alive = survival(layer, 1, mortal, crowding)
                wet = state[cohort, layer] * alive
                wet_edge[0, layer, spot, :] = wet[:1]
                wet_edge[1, layer, spot, :] = wet[rows - 1 :]
                before = from_before(wet, 0.0)
                after = from_after(wet, 0.0)
                west_val = rolled(wet, 1, 1)
                east_val = rolled(wet, -1, 1)
                adjoint = cot[cohort, layer]
                swum = swim * adjoint
                products.append(
                    (
                        swum * (east_val - west_val),
                        swum * (after - before),
                        adjoint * ((before + after) + (west_val + east_val) - 4.0 * wet),
                    )
                )
                pull = pulled(adjoint, swum, layer, spot)
                kept[cohort, layer] = pull * alive
                added.append(crowding * (pull * wet))
            for index in range(3):
                grads[index, layer] += added_up([product[index] for product in products])
            return sums - added_up(added)

        partial[2, layer] = over_cohorts(back2)
        begin(exchange(2, layer))

    def second_beyond(layer):
        receive(CROWD2, layer)
        receive(COT2, layer)

        def back2_halo(first, spot):
            swim = wide(3, first)
            for side in range(2):
                sign = 1.0 if side == 0 else -1.0
                adjoint = cot1_h[side, layer, spot, :]
                behind = cot2_h[side, layer, spot, :]
                ours = cot1_o[side, layer, spot, :]
                swum = swim * adjoint
                spread_out = halo_row(side, KAPPA, 0, layer) * adjoint
                drift = halo_row(side, EAST, 0, layer) * swum
                outer_coef = halo_row(side, KAPPA, 1, layer) - sign * swim * halo_row(side, NORTH, 1, layer)
                inner_coef = spread(field[KAPPA, layer, inner(side), :]) + sign * swim * spread(
                    field[NORTH, layer, inner(side), :]
                )
                pull = (
                    halo_row(side, CENTRE, 0, layer) * adjoint
                    + rolled(spread_out - drift, 1, 1)
                    + rolled(spread_out + drift, -1, 1)
                    + outer_coef * behind
                    + inner_coef * ours
                )
                alive = survival_h(side, first, layer)
                kept_h[side, layer, spot, :] = pull * alive
                added = inflow[side, layer, spot, :] * alive
                west_val = rolled(added, 1, 1)
                east_val = rolled(added, -1, 1)
                wet = wet_edge[side, layer, spot, :]
                beyond[1, side, layer] -= wide(1, first) * (pull * added)
                edge_sum[side, KAPPA_NEAR, layer] += adjoint * (wet + (west_val + east_val) - 4.0 * added)
                edge_sum[side, NORTH_NEAR, layer] += swum * wet
                edge_sum[side, EAST_NEAR, layer] += swum * (east_val - west_val)
                edge_sum[side, KAPPA_FAR, layer] += behind * added
                edge_sum[side, NORTH_FAR, layer] += swim * (behind * added)
                edge_sum[side, KAPPA_OWN, layer] += ours * added
                edge_sum[side, NORTH_OWN, layer] += swim * (ours * added)

        over_groups(back2_halo)
        for side in range(2):
            beyond_o[layer, side : side + 1, :] = column(beyond[1, side, layer])
        begin(exchange_beyond(layer))

    def second_pressure(layer):
        summed(2, layer)
        for copy in exchange_beyond(layer):
            copy.wait_recv()
        value = beyond_o[layer]
        for by in range(n_coh - 1):
            value = value + beyond_in[by, layer]
        value = value * (1.0 / every)
        outside[layer] = value
        for side in range(2):
            press_o[side, layer, :1] = total[2, layer, inner(side), :]
            press_o[side, layer, 1:] = value[side : side + 1]
        send(PRESS2, layer)

    def first_back(layer):
        receive(PRESS2, layer)
        total[2, layer] += jnp.where(is_first, press_h[0, layer, 1:], 0.0) + jnp.where(
            is_last, press_h[1, layer, 1:], 0.0
        )

        def inflow_first(first, spot):
            swim = wide(3, first)
            for side in range(2):
                pressure = press_h[side, layer, :1] + outside[layer, side : side + 1]
                adjoint = kept_h[side, layer, spot, :] + wide(2, first) * spread(pressure)
                into[side, layer, spot, :] = coefs[side, layer, spot, :] * adjoint
                product = adjoint * wet1_edge[side, layer, spot, :]
                edge_sum[side, KAPPA_NEAR, layer] += product
                edge_sum[side, NORTH_NEAR, layer] += swim * product

        over_groups(inflow_first)
        for side in range(2):
            for index in range(SENT):
                edge_o[side, layer, index : index + 1] = column(edge_sum[side, index, layer])
        send(EDGE, layer)

        def back1(group, sums):
            added = []
            products = []
            for cohort in group:
                mortal, crowding, weight, swim = scalars(cohort)
                adjoint = kept[cohort, layer] + weight * total[2, layer]
                swum = swim * adjoint
                products.append(
                    (
                        swum * east1[cohort, layer],
                        swum * north1[cohort, layer],
                        adjoint * lap1[cohort, layer],
                    )
                )
                pull = pulled(adjoint, swum, layer, pl.ds(cohort, 1))
                last[cohort, layer] = pull * surv1[cohort, layer]
                added.append(crowding * (pull * wet1[cohort, layer]))
            for index in range(3):
                grads[index, layer] += added_up([product[index] for product in products])
            return sums - added_up(added)

        partial[3, layer] = over_cohorts(back1)
        begin(exchange(3, layer))

    def put(layer):
        return [
            pltpu.make_async_copy(
                last.at[pl.ds(at * chunk, chunk), layer],
                out.at[pl.ds(at * chunk, chunk), layer],
                local_sem.at[2 + layer, at],
            )
            for at in range(CHUNKS)
        ]

    part = lon // n_coh

    def gradients(layer):
        receive(EDGE, layer)
        ocean = field[OCEAN, layer]
        near = (is_first, is_last)
        behind = (row == 1, row == rows - 2)
        drift, climb, kappa = (grads[index, layer] for index in range(3))
        for side in range(2):

            def got(index):
                return edge_h[side, layer, index : index + 1, :]

            sign = -1.0 if side == 0 else 1.0
            kappa_near = got(KAPPA_NEAR) + column(edge_sum[side, KAPPA_OWN, layer])
            north_near = sign * (got(NORTH_NEAR) + column(edge_sum[side, NORTH_OWN, layer]))
            drift = drift + jnp.where(near[side], got(EAST_NEAR), 0.0)
            climb = climb + jnp.where(near[side], north_near, 0.0)
            climb = climb + jnp.where(behind[side], sign * got(NORTH_FAR), 0.0)
            kappa = kappa + jnp.where(near[side], kappa_near, 0.0)
            kappa = kappa + jnp.where(behind[side], got(KAPPA_FAR), 0.0)
        values = (-0.5 * ocean * drift, -0.5 * ocean * climb, ocean * kappa)
        for index, value in enumerate(values):
            for to in range(n_coh):
                share[to, layer, index] = value[:, to * part : (to + 1) * part]
        begin(exchange_share(layer))

    for layer in range(layers):
        first_step(layer)
    for layer in range(layers):
        second_back(layer)
        if layer > 0:
            second_pressure(layer - 1)
        second_beyond(layer)
    for layer in range(layers):
        if layer == layers - 1:
            second_pressure(layer)
        if layer > 0:
            gradients(layer - 1)
        first_back(layer)
        begin(put(layer))
    gradients(layers - 1)
    for layer in range(layers):
        summed(3, layer)
        out_press[layer] = total[3, layer]
        for copy in exchange_share(layer):
            copy.wait_recv()
        for index in range(3):
            value = share[coh, layer, index]
            for by in range(n_coh - 1):
                value = value + share_in[by, layer, index]
            out_grads[index, layer] = value

    for layer in range(layers):
        for copy in put(layer):
            copy.wait()
        for kind in buffers:
            sent(kind, layer)
        for which in range(2 * STEPS):
            for copy in exchange(which, layer):
                copy.wait_send()
        for copy in exchange_beyond(layer) + exchange_share(layer):
            copy.wait_send()


def finish(age, mass, last, press, grads, out, out_east, out_north, out_kappa, held, sem):
    cohorts, layers = held.shape[:2]
    chunk = cohorts // CHUNKS
    spots = [pl.ds(at * chunk, chunk) for at in range(CHUNKS)]
    get = [
        pltpu.make_async_copy(last.at[spot], held.at[spot], sem.at[0, at])
        for at, spot in enumerate(spots)
    ]
    put = [
        pltpu.make_async_copy(held.at[spot], out.at[spot], sem.at[1, at])
        for at, spot in enumerate(spots)
    ]
    for copy in get:
        copy.start()
    for index, target in enumerate((out_east, out_north, out_kappa)):
        target[...] = grads[index]
    for at in range(CHUNKS):
        get[at].wait()
        for cohort in range(at * chunk, (at + 1) * chunk):
            weight = mass[age[cohort]]
            for layer in range(layers):
                held[cohort, layer] += weight * press[layer]
        put[at].start()
    for copy in put:
        copy.wait()


def local(*args):
    density = args[0]
    cohorts, layers, rows, lon = density.shape
    n_lat, n_coh = lax.axis_size("lat"), lax.axis_size("coh")
    f32 = jnp.float32
    vmem = pl.BlockSpec(memory_space=pltpu.VMEM)
    smem = pl.BlockSpec(memory_space=pltpu.SMEM)
    share = jax.ShapeDtypeStruct((layers, rows, lon // n_coh), f32)
    whole = pltpu.VMEM(density.shape, f32)
    packed = pltpu.VMEM((2, layers, cohorts, lon), f32)
    def vec(*shape):
        return pltpu.VMEM(shape, f32)

    part = lon // n_coh
    hbm = pl.BlockSpec(memory_space=pl.ANY)
    scratch = (
        [whole] * 3
        + [
            vec(5, layers, rows, lon),
            vec(2, layers, 10, lon),
            vec(4, cohorts, 128),
        ]
        + [whole] * 7
        + [
            vec(4, layers, rows, lon),
            vec(4, layers, rows, lon),
            vec(4, n_coh - 1, layers, rows, lon),
            vec(3, layers, rows, lon),
            vec(n_coh, layers, 3, rows, part),
            vec(n_coh - 1, layers, 3, rows, part),
            packed,
            vec(2, layers, 8, lon),
            vec(2, layers, 8, lon),
            packed,
            packed,
            packed,
            packed,
            vec(2, layers, 1, lon),
            vec(2, layers, 1, lon),
            vec(2, layers, 1, lon),
            vec(2, layers, 1, lon),
            vec(2, layers, 2, lon),
            vec(2, layers, 2, lon),
            vec(2, layers, SENT, lon),
            vec(2, layers, SENT, lon),
            vec(2, 7, layers, 8, lon),
            vec(2, 2, layers, 8, lon),
            vec(layers, 2, lon),
            vec(n_coh - 1, layers, 2, lon),
            vec(layers, 2, lon),
        ]
        + [packed] * 6
        + [
            pltpu.SemaphoreType.DMA((2 + layers, CHUNKS)),
            pltpu.SemaphoreType.DMA((7, layers, 2)),
            pltpu.SemaphoreType.DMA((7, layers, 2)),
            pltpu.SemaphoreType.DMA((6, layers, n_coh - 1)),
            pltpu.SemaphoreType.DMA((6, layers, n_coh - 1)),
        ]
    )
    size = density.size
    last, press, grads = pl.pallas_call(
        functools.partial(kernel, n_lat, n_coh),
        out_shape=(
            jax.ShapeDtypeStruct(density.shape, f32),
            jax.ShapeDtypeStruct((layers, rows, lon), f32),
            jax.ShapeDtypeStruct((3, layers, rows, part), f32),
        ),
        in_specs=[hbm] * 2 + [vmem] * 4 + [smem] * 5,
        out_specs=(hbm, vmem, vmem),
        scratch_shapes=scratch,
        compiler_params=pltpu.CompilerParams(
            collective_id=0, has_side_effects=True, vmem_limit_bytes=56 * 1024 * 1024
        ),
        cost_estimate=pl.CostEstimate(
            flops=150 * size, bytes_accessed=12 * size, transcendentals=2 * size
        ),
    )(*args)
    return pl.pallas_call(
        finish,
        out_shape=(jax.ShapeDtypeStruct(density.shape, f32), share, share, share),
        in_specs=[smem, smem, hbm, vmem, vmem],
        out_specs=(hbm, vmem, vmem, vmem),
        scratch_shapes=[whole, pltpu.SemaphoreType.DMA((2, CHUNKS))],
        compiler_params=pltpu.CompilerParams(vmem_limit_bytes=56 * 1024 * 1024),
        cost_estimate=pl.CostEstimate(flops=2 * size, bytes_accessed=8 * size, transcendentals=0),
    )(args[6], args[9], last, press, grads)


def solution(mesh):
    fields = P(None, "lat", None)
    in_specs = (P("coh", None, "lat", None),) * 2 + (fields,) * 4 + (P("coh"),) + (P(),) * 4
    out_specs = (P("coh", None, "lat", None),) + (P(None, "lat", "coh"),) * 3
    return jax.shard_map(local, mesh=mesh, in_specs=in_specs, out_specs=out_specs, check_vma=False)
```
